256 devices in a mesh: seq: 32 (over y, z), blk: 8 (over x, core).
Axes of the slice: x: 4, y: 4, z: 8, core: 2. Of those that a mesh axis runs over, the one named last changes fastest.
Arguments:
- teacher_query: bfloat16 [8, 1024, 4096], P('blk', 'seq'), may hold values from -6 to 6
- teacher_key: bfloat16 [8, 1024, 4096], P('blk', 'seq'), may hold values from -6 to 6
- teacher_value: bfloat16 [8, 1024, 4096], P('blk', 'seq'), may hold values from -6 to 6
- student_query: bfloat16 [8, 1024, 4096], P('blk', 'seq'), may hold values from -6 to 6
- student_key: bfloat16 [8, 1024, 4096], P('blk', 'seq'), may hold values from -6 to 6
- student_value: bfloat16 [8, 1024, 4096], P('blk', 'seq'), may hold values from -6 to 6
- frame_index: int32 [8, 1024], P('blk', 'seq'), may hold values from 0 to 6, as said below
Outputs:
- query_grad: bfloat16 [8, 1024, 4096], P('blk', 'seq')
- key_grad: bfloat16 [8, 1024, 4096], P('blk', 'seq')
- value_grad: bfloat16 [8, 1024, 4096], P('blk', 'seq')
The draws below stay inside these ranges and needn't reach their ends.
Inputs may be any that keep to these rules, and one draw needn't show every extreme that they name: `frame_index`: read row after row, frame numbers never fall; every frame 0 to 6 holds at least (6144) // 6 - 6144 // 24 tokens and at most 2048, and one frame holds exactly 2048.
All inputs are finite; a program needn't handle non-finite values.
Results may differ from the reference program's by a relative error of at most 0.028.
Values may be sent and summed in bfloat16 or wider, within the bound.
No kernel may reach another device: no remote copies, remote signals or barrier semaphores. Data moves between devices by JAX's collectives and lax.ppermute only.
A program may use at most 64 MiB of HBM per device.

```python
import math
import jax
import jax.numpy as jnp
from jax import lax

HEADS = 32
DH = 128
FRAMES = 7
HD = 4096
GROUP_TOK = 1024
GROUPS = 8
TOKENS = 8192


def drawn_rows(key):
    return jnp.clip(jax.random.normal(key, (TOKENS, HD), jnp.float32), -6.0, 6.0)


def shaped(matrix):
    return matrix.reshape(GROUPS, GROUP_TOK, HD).astype(jnp.bfloat16)


def draw_teacher_query(key, part):
    key = jax.random.fold_in(key, 1)
    return shaped(drawn_rows(key))


def draw_teacher_key(key, part):
    key = jax.random.fold_in(key, 2)
    return shaped(drawn_rows(key))


def draw_student_query(key, part):
    key = jax.random.fold_in(key, 3)
    return shaped(drawn_rows(key))


def draw_student_key(key, part):
    key = jax.random.fold_in(key, 4)
    return shaped(drawn_rows(key))


def draw_frame_index(key, part):
    key = jax.random.fold_in(key, 5)
    first_key, second_key = jax.random.split(key)
    largest = TOKENS // 4
    remaining = TOKENS - largest
    others = FRAMES - 1
    jitter = jax.random.randint(first_key, (others,), 0, remaining // 24 + 1)
    pieces = remaining // others + jitter - jnp.roll(jitter, 1)
    pieces = pieces.at[others - 1].add(remaining - others * (remaining // others))
    chosen = jax.random.randint(second_key, (), 0, FRAMES)
    slots = jnp.arange(FRAMES)
    before = pieces[jnp.clip(slots, 0, others - 1)]
    after = pieces[jnp.clip(slots - 1, 0, others - 1)]
    lengths = jnp.where(slots < chosen, before, jnp.where(slots == chosen, largest, after))
    ends = jnp.cumsum(lengths)
    positions = jnp.arange(TOKENS)
    frames = jnp.sum((positions[:, None] >= ends[None, :]).astype(jnp.int32), axis=1)
    return frames.astype(jnp.int32).reshape(GROUPS, GROUP_TOK)


def level_of(key, extent, cuts, low, high):
    level = 1.0
    for axis_at, blocks in cuts:
        steps = jax.random.uniform(jax.random.fold_in(jax.random.fold_in(key, 6), axis_at), (blocks,), jnp.float32, low / len(cuts), high / len(cuts))
        level = level * jnp.repeat(jnp.exp(steps), extent[axis_at] // blocks).reshape((-1,) + (1,) * (len(extent) - 1 - axis_at))
    return level


def noise(stream_key, extent, width, reach, shards=(), kind=jnp.bfloat16):
    result = jax.random.normal(stream_key, extent, jnp.float32) * width
    if len(shards) > 0:
        result = level_of(stream_key, extent, shards, -0.22, 0.18) * result
    return jnp.clip(result, min=-reach, max=reach).astype(kind)


def setup_inputs(seed: int = 0) -> dict:
    key_list = jax.random.split(jax.random.key(seed), 8)
    return {
        "teacher_query": draw_teacher_query(jax.random.fold_in(key_list[7], 71), 0),
        "teacher_key": draw_teacher_key(jax.random.fold_in(key_list[7], 71), 0),
        "teacher_value": noise(key_list[2], (GROUPS, GROUP_TOK, HD), 1.0, 6.0, ((0, 8), (1, 32))),
        "student_query": draw_student_query(jax.random.fold_in(key_list[7], 71), 0),
        "student_key": draw_student_key(jax.random.fold_in(key_list[7], 71), 0),
        "student_value": noise(key_list[5], (GROUPS, GROUP_TOK, HD), 1.0, 6.0, ((0, 8), (1, 32))),
        "frame_index": draw_frame_index(jax.random.fold_in(key_list[7], 71), 0),
    }


loss_scale = 64.0


def head_gradients(t_query, t_key, t_value, s_query, s_key, s_value, frames):
    factor = DH ** -0.5
    row_block = math.gcd(TOKENS, 512)

    def advance(carried, block_index):
        key_sum, value_sum = carried
        first_row = block_index * row_block
        t_rows = lax.dynamic_slice_in_dim(t_query, first_row, row_block)
        s_rows = lax.dynamic_slice_in_dim(s_query, first_row, row_block)
        row_frames = lax.dynamic_slice_in_dim(frames, first_row, row_block)
        scores = jnp.dot(t_rows, t_key.T, preferred_element_type=jnp.float32) * factor
        maxima = jnp.max(scores, axis=1)
        weights = jnp.exp(scores - maxima[:, None])
        totals = jnp.sum(weights, axis=1)
        target = (jnp.dot(weights.astype(jnp.bfloat16), t_value, preferred_element_type=jnp.float32) / totals[:, None]).astype(jnp.bfloat16)
        visible = frames[None, :] <= row_frames[:, None]
        scores = jnp.dot(s_rows, s_key.T, preferred_element_type=jnp.float32) * factor
        maxima = jnp.max(jnp.where(visible, scores, -jnp.inf), axis=1)
        weights = jnp.where(visible, jnp.exp(scores - maxima[:, None]), 0.0)
        totals = jnp.sum(weights, axis=1)
        output = jnp.dot(weights.astype(jnp.bfloat16), s_value, preferred_element_type=jnp.float32) / totals[:, None]
        out_grad = (loss_scale * (output - target.astype(jnp.float32))).astype(jnp.bfloat16)
        deltas = jnp.sum(out_grad.astype(jnp.float32) * output, axis=1)
        attention = jnp.where(visible, jnp.exp(scores - maxima[:, None]) / totals[:, None], 0.0)
        attention_grad = jnp.dot(out_grad, s_value.T, preferred_element_type=jnp.float32)
        score_grad = (attention * (attention_grad - deltas[:, None]) * factor).astype(jnp.bfloat16)
        query_rows = jnp.dot(score_grad, s_key, preferred_element_type=jnp.float32).astype(jnp.bfloat16)
        key_sum = key_sum + jnp.dot(score_grad.T, s_rows, preferred_element_type=jnp.float32)
        value_sum = value_sum + jnp.dot(attention.astype(jnp.bfloat16).T, out_grad, preferred_element_type=jnp.float32)
        return (key_sum, value_sum), query_rows

    initial = (jnp.zeros((TOKENS, DH), jnp.float32), jnp.zeros((TOKENS, DH), jnp.float32))
    (key_sum, value_sum), query_blocks = lax.scan(advance, initial, jnp.arange(TOKENS // row_block, dtype=jnp.int32))
    return query_blocks.reshape(TOKENS, DH), key_sum.astype(jnp.bfloat16), value_sum.astype(jnp.bfloat16)


def reference(teacher_query, teacher_key, teacher_value, student_query, student_key, student_value, frame_index):
    def by_head(matrix):
        return matrix.reshape(TOKENS, HEADS, DH).transpose(1, 0, 2)

    frames = frame_index.reshape(TOKENS)
    inputs = tuple(by_head(member) for member in (teacher_query, teacher_key, teacher_value, student_query, student_key, student_value))
    results = lax.map(lambda head_arrays: head_gradients(*head_arrays, frames), inputs)

    def by_token(stacked):
        return stacked.transpose(1, 0, 2).reshape(GROUPS, GROUP_TOK, HD)

    return by_token(results[0]), by_token(results[1]), by_token(results[2])
```

```python
import functools

import jax
import jax.numpy as jnp
from jax import lax
from jax.experimental import pallas as pl
from jax.experimental.pallas import tpu as pltpu
from jax.sharding import PartitionSpec as P

DH = 128
HEADS = 32
SHARD = 32
ROWS = 1024
HALF = 512
TOKENS = 8192
EXTRA = 16
scale = DH ** -0.5
scale_log2 = scale * 1.4426950408889634
loss_scale = 64.0
hidden_bias = -131072.0
AXES = ("blk", "seq")
SETS = [[(j if s < 16 else 7 - j) * 32 + s for s in range(32)] for j in range(8)]
f32 = jnp.float32
bf16 = jnp.bfloat16
VMEM = pl.BlockSpec(memory_space=pltpu.VMEM)
SMEM = pl.BlockSpec(memory_space=pltpu.SMEM)
ANY = pl.BlockSpec(memory_space=pl.ANY)


def params():
    return pltpu.CompilerParams(vmem_limit_bytes=60 * 2**20)


def dot(a, b):
    return jnp.dot(a, b, preferred_element_type=f32)


def pack_queries_kernel(first_ref, second_ref, counts_ref, out_ref):
    for h in range(HEADS):
        cols = slice(h * DH, (h + 1) * DH)
        out_ref[h, :SHARD, :DH] = first_ref[:, cols]
        out_ref[h, :SHARD, DH:] = second_ref[:, cols]
        out_ref[h, SHARD:, :] = counts_ref[...]


def pack_queries(first, second, counts):
    return pl.pallas_call(
        pack_queries_kernel,
        out_shape=jax.ShapeDtypeStruct((HEADS, SHARD + EXTRA, 2 * DH), bf16),
        in_specs=[VMEM] * 3,
        out_specs=VMEM,
        compiler_params=params(),
    )(first, second, counts)


def pack_four_kernel(a_ref, b_ref, c_ref, d_ref, out_ref):
    for h in range(HEADS):
        cols = slice(h * DH, (h + 1) * DH)
        out_ref[h, :SHARD, :DH] = a_ref[:, cols]
        out_ref[h, :SHARD, DH:] = b_ref[:, cols]
        out_ref[h, SHARD:, :DH] = c_ref[:, cols]
        out_ref[h, SHARD:, DH:] = d_ref[:, cols]


def pack_four(a, b, c, d):
    return pl.pallas_call(
        pack_four_kernel,
        out_shape=jax.ShapeDtypeStruct((HEADS, 2 * SHARD, 2 * DH), bf16),
        in_specs=[VMEM] * 4,
        out_specs=VMEM,
        compiler_params=params(),
    )(a, b, c, d)


def unpack_one_kernel(in_ref, out_ref):
    for h in range(HEADS):
        out_ref[:, h * DH:(h + 1) * DH] = in_ref[h]


def unpack_one(rows):
    return pl.pallas_call(
        unpack_one_kernel,
        out_shape=jax.ShapeDtypeStruct((SHARD, HEADS * DH), bf16),
        in_specs=[VMEM],
        out_specs=VMEM,
        compiler_params=params(),
    )(rows)


def unpack_two_kernel(in_ref, first_ref, second_ref):
    for h in range(HEADS):
        cols = slice(h * DH, (h + 1) * DH)
        first_ref[:, cols] = in_ref[h, :, :DH]
        second_ref[:, cols] = in_ref[h, :, DH:]


def unpack_two(rows):
    return pl.pallas_call(
        unpack_two_kernel,
        out_shape=[jax.ShapeDtypeStruct((SHARD, HEADS * DH), bf16)] * 2,
        in_specs=[VMEM],
        out_specs=[VMEM] * 2,
        compiler_params=params(),
    )(rows)


def fold(op, x):
    return op(x.reshape(-1, 8, x.shape[-1]), axis=0)


def online_step(scores, values_t, cols, max_ref, sum_ref, out_ref):
    before = max_ref[0:1, cols]
    highest = jnp.max(fold(jnp.max, scores), axis=0, keepdims=True) * scale_log2
    now = jnp.maximum(before, highest)
    shrink = jnp.exp2(before - now)
    weights = jnp.exp2(scores * scale_log2 - now)
    rounded = weights.astype(bf16)
    block_sum = jnp.sum(fold(jnp.sum, weights), axis=0, keepdims=True)
    sum_ref[0:1, cols] = sum_ref[0:1, cols] * shrink + block_sum
    out_ref[:, cols] = out_ref[:, cols] * shrink + dot(values_t, rounded)
    max_ref[0:1, cols] = now
    return rounded, now


def clear(max_ref, sum_ref, out_ref):
    max_ref[...] = jnp.full(max_ref.shape, -1e30, f32)
    sum_ref[...] = jnp.zeros(sum_ref.shape, f32)
    out_ref[...] = jnp.zeros(out_ref.shape, f32)


def load_pieces(pieces, held, sems):
    copies = [
        pltpu.make_async_copy(piece, held.at[pl.ds(i * ROWS, ROWS)], sems.at[i])
        for i, piece in enumerate(pieces)
    ]
    for copy in copies:
        copy.start()
    return copies


def take_queries(q_ref, meta_ref, cols):
    parts = []
    for h in range(2):
        at = pl.ds(meta_ref[10 + h], SHARD // 2)
        parts.append(q_ref[at, :SHARD, cols].reshape(HALF, DH))
    return jnp.concatenate(parts, axis=0)


def rows_of(i):
    return pl.ds(pl.multiple_of(i * ROWS, ROWS), ROWS)


def teacher_kernel(meta_ref, q_ref, *rest):
    pieces = rest[:8]
    target_ref, held, max_ref, sum_ref, out_ref, sems = rest[8:]
    copies = load_pieces(pieces, held, sems)
    clear(max_ref, sum_ref, out_ref)
    queries_t = take_queries(q_ref, meta_ref, slice(0, DH)).T
    for copy in copies:
        copy.wait()

    def step(i, _):
        rows = rows_of(i)
        scores = dot(held[rows, :DH], queries_t)
        online_step(scores, held[rows, DH:].T, slice(0, ROWS), max_ref, sum_ref, out_ref)
        return 0

    lax.fori_loop(0, 8, step, 0)
    target_ref[...] = (out_ref[...] / sum_ref[0:1, :]).astype(bf16)


def teacher(meta, queries, pieces):
    return pl.pallas_call(
        teacher_kernel,
        out_shape=jax.ShapeDtypeStruct((DH, ROWS), bf16),
        in_specs=[SMEM, VMEM] + [ANY] * 8,
        out_specs=VMEM,
        scratch_shapes=[
            pltpu.VMEM((TOKENS, 2 * DH), bf16),
            pltpu.VMEM((8, ROWS), f32),
            pltpu.VMEM((8, ROWS), f32),
            pltpu.VMEM((DH, ROWS), f32),
            pltpu.SemaphoreType.DMA((8,)),
        ],
        compiler_params=params(),
        cost_estimate=pl.CostEstimate(
            flops=16 * 10**9, bytes_accessed=6 * 2**20, transcendentals=ROWS * TOKENS
        ),
    )(meta, queries, *pieces)


def frames_of(tokens, meta_ref):
    frames = jnp.zeros(tokens.shape, jnp.int32)
    for f in range(6):
        frames = frames + (tokens >= meta_ref[f]).astype(jnp.int32)
    return frames


def groups_seen(meta_ref, last):
    seen = jnp.int32(TOKENS)
    for f in range(6, -1, -1):
        seen = jnp.where(last < meta_ref[f], meta_ref[f], seen)
    return (seen + (ROWS - 1)) // ROWS


def keys_with_frames(keys, group, meta_ref):
    column = lax.broadcasted_iota(jnp.int32, (ROWS, DH), 1)
    tokens = group * ROWS + lax.broadcasted_iota(jnp.int32, (ROWS, DH), 0)
    one_hot = (frames_of(tokens, meta_ref) == column).astype(f32).astype(bf16)
    return jnp.concatenate([keys, one_hot], axis=1)


def by_visibility(meta_ref, group, compute, skip=None):
    seen_early = groups_seen(meta_ref, meta_ref[8] + (HALF - 1))
    seen_late = groups_seen(meta_ref, meta_ref[9] + (HALF - 1))

    @pl.when(group < seen_early)
    def _():
        compute(0)

    @pl.when((group >= seen_early) & (group < seen_late))
    def _():
        compute(HALF)

    if skip is not None:

        @pl.when(group >= seen_late)
        def _():
            skip()


def student_kernel(meta_ref, q_ref, target_ref, *rest):
    pieces = rest[:8]
    dq_ref = rest[8]
    outs = rest[9:15]
    held, max_ref, sum_ref, out_ref, weights_ref, max_at, dqt, qt_ref, kv_grad, sems, out_sems = rest[15:]
    copies = load_pieces(pieces, held, sems)
    clear(max_ref, sum_ref, out_ref)
    dqt[...] = jnp.zeros(dqt.shape, f32)
    queries = take_queries(q_ref, meta_ref, slice(DH, 2 * DH))
    column = lax.broadcasted_iota(jnp.int32, (DH, ROWS), 1)
    row = lax.broadcasted_iota(jnp.int32, (DH, ROWS), 0)
    tokens = jnp.where(column < HALF, meta_ref[8] + column, meta_ref[9] + (column - HALF))
    bias = jnp.where((row > frames_of(tokens, meta_ref)) & (row < 7), hidden_bias, 0.0)
    qt_ref[:DH, :] = queries.T
    qt_ref[DH:, :] = bias.astype(bf16)
    for copy in copies:
        copy.wait()

    def forward(i, _):
        group = meta_ref[16 + i]

        def compute(first):
            rows, cols = rows_of(i), slice(first, ROWS)
            keys = keys_with_frames(held[rows, :DH], group, meta_ref)
            rounded, now = online_step(
                dot(keys, qt_ref[:, cols]), held[rows, DH:].T, cols, max_ref, sum_ref, out_ref
            )
            weights_ref[rows, cols] = rounded
            at = pl.ds(pl.multiple_of(i * 8, 8), 8)
            max_at[at, cols] = jnp.broadcast_to(now, (8, ROWS - first))

        by_visibility(meta_ref, group, compute)
        return 0

    lax.fori_loop(0, 8, forward, 0)

    inverse = 1.0 / sum_ref[0:1, :]
    output = out_ref[...] * inverse
    out_grad = (loss_scale * (output - target_ref[...].astype(f32))).astype(bf16).astype(f32)
    delta = jnp.sum(out_grad * output, axis=0, keepdims=True) * inverse
    grad_t = (out_grad * inverse).astype(bf16)
    delta_1 = delta.astype(bf16).astype(f32)
    delta_2 = (delta - delta_1).astype(bf16).astype(f32)
    delta_3 = delta - delta_1 - delta_2
    delta_rows = jnp.where(
        row == 0, -delta_1, jnp.where(row == 1, -delta_2, jnp.where(row == 2, -delta_3, 0.0))
    )
    grad_delta_t = jnp.concatenate([grad_t, delta_rows.astype(bf16)], axis=0)
    grad = grad_t.T
    key_column = lax.broadcasted_iota(jnp.int32, (ROWS, DH), 1)
    ones = jnp.where(key_column < 3, 1.0, 0.0).astype(bf16)

    def backward(i, _):
        group = meta_ref[16 + i]

        def compute(first):
            rows, cols = rows_of(i), slice(first, ROWS)
            values = jnp.concatenate([held[rows, DH:], ones], axis=1)
            centred = dot(values, grad_delta_t[:, cols])
            at = pl.ds(pl.multiple_of(i * 8, 8), 8)
            shrink = jnp.exp2(max_at[at, cols][0:1] - max_ref[0:1, cols])
            weights = weights_ref[rows, cols].astype(f32) * shrink
            score_grad = (weights * centred).astype(bf16)
            kv_grad[rows, DH:] = dot(weights.astype(bf16), grad[cols]).astype(bf16)
            kv_grad[rows, :DH] = (dot(score_grad, queries[cols]) * scale).astype(bf16)
            dqt[:, cols] += dot(held[rows, :DH].T, score_grad)

        def skip():
            kv_grad[rows_of(i), :] = jnp.zeros((ROWS, 2 * DH), bf16)

        by_visibility(meta_ref, group, compute, skip)
        return 0

    lax.fori_loop(0, 8, backward, 0)
    out_copies = [
        pltpu.make_async_copy(kv_grad.at[pl.ds(i * ROWS, ROWS)], out, out_sems.at[k])
        for k, (i, out) in enumerate(
            [(0, outs[0]), (1, outs[1]), (2, outs[2].at[0]), (4, outs[2].at[1])]
            + [(3, outs[3].at[0]), (5, outs[3].at[1]), (6, outs[4]), (7, outs[5])]
        )
    ]
    for copy in out_copies:
        copy.start()
    query_grad = (dqt[...] * scale).T.astype(bf16)
    for h in range(2):
        at = pl.ds(pl.multiple_of(meta_ref[10 + h] * SHARD, HALF), HALF)
        dq_ref[at, :] = query_grad[h * HALF:(h + 1) * HALF]
    for copy in out_copies:
        copy.wait()


def student(meta, queries, target, pieces):
    one = jax.ShapeDtypeStruct((ROWS, 2 * DH), bf16)
    two = jax.ShapeDtypeStruct((2, ROWS, 2 * DH), bf16)
    return pl.pallas_call(
        student_kernel,
        out_shape=[jax.ShapeDtypeStruct((ROWS, DH), bf16), one, one, two, two, one, one],
        in_specs=[SMEM, VMEM, VMEM] + [ANY] * 8,
        out_specs=[VMEM] + [ANY] * 6,
        scratch_shapes=[
            pltpu.VMEM((TOKENS, 2 * DH), bf16),
            pltpu.VMEM((8, ROWS), f32),
            pltpu.VMEM((8, ROWS), f32),
            pltpu.VMEM((DH, ROWS), f32),
            pltpu.VMEM((TOKENS, ROWS), bf16),
            pltpu.VMEM((64, ROWS), f32),
            pltpu.VMEM((DH, ROWS), f32),
            pltpu.VMEM((2 * DH, ROWS), bf16),
            pltpu.VMEM((TOKENS, 2 * DH), bf16),
            pltpu.SemaphoreType.DMA((8,)),
            pltpu.SemaphoreType.DMA((8,)),
        ],
        compiler_params=params(),
        cost_estimate=pl.CostEstimate(
            flops=26 * 10**9, bytes_accessed=10 * 2**20, transcendentals=ROWS * TOKENS
        ),
    )(meta, queries, target, *pieces)


def exchange(packed, sets):
    return lax.all_to_all(
        packed, AXES, split_axis=0, concat_axis=0, tiled=True, axis_index_groups=sets
    )


def exchange_groups(packed):
    return lax.all_to_all(packed, "seq", split_axis=0, concat_axis=0, tiled=True)


def chip_shift(x, by):
    return lax.ppermute(x, "blk", [(i, ((i // 2 + by) % 4) * 2 + i % 2) for i in range(8)])


def swap_cores(x):
    return lax.ppermute(x, "blk", [(i, i ^ 1) for i in range(8)])


def chip_blocks(own):
    return [own] + [chip_shift(own, by) for by in (3, 1, 2)]


def with_other_core(parts):
    return [x for part in parts for x in (part, swap_cores(part))]


def frame_ends(counted):
    counts = jnp.broadcast_to(jnp.sum(counted.astype(f32), axis=0)[:, None], (8, DH))
    counts = counts + swap_cores(counts)
    counts = counts + chip_shift(counts, 1)
    counts = counts + chip_shift(counts, 2)
    return counts[:, 0].astype(jnp.int32)


def per_device(
    teacher_query,
    teacher_key,
    teacher_value,
    student_query,
    student_key,
    student_value,
    frame_index,
):
    blk = lax.axis_index("blk")
    seq = lax.axis_index("seq")
    keys_values = exchange_groups(
        pack_four(teacher_key[0], teacher_value[0], student_key[0], student_value[0])
    )
    teacher_kv = keys_values[:, :SHARD].reshape(ROWS, 2 * DH)
    teacher_parts = chip_blocks(teacher_kv)
    teacher_pieces = with_other_core(teacher_parts)
    teacher_query, keys_values = lax.optimization_barrier((teacher_query, keys_values))
    student_kv = keys_values[:, SHARD:].reshape(ROWS, 2 * DH)
    student_kv, _ = lax.optimization_barrier((student_kv, teacher_parts[3]))
    frame_ids = jnp.arange(2 * DH, dtype=jnp.int32)
    counts = jnp.sum((frame_index[0][:, None] <= frame_ids[None, :]).astype(f32), axis=0)
    counts = jnp.broadcast_to(counts.astype(bf16), (EXTRA, 2 * DH))
    queries = exchange(pack_queries(teacher_query[0], student_query[0], counts), SETS)
    ends = frame_ends(queries[:, SHARD, :8])
    student_parts = chip_blocks(student_kv)

    chip, core = blk // 2, blk % 2
    own_set = jnp.where(seq < 16, blk, 7 - blk)
    low, high = own_set * ROWS, (7 - own_set) * ROWS + HALF
    groups = []
    for by in (0, 1, 3, 2):
        groups += [((chip + by) % 4) * 2 + core, ((chip + by) % 4) * 2 + 1 - core]
    halves = jnp.stack([jnp.minimum(low, high), jnp.maximum(low, high)])
    members = jnp.where(low < high, jnp.array([0, SHARD // 2]), jnp.array([SHARD // 2, 0]))
    place = [halves, members, jnp.zeros((4,), jnp.int32), jnp.stack(groups)]
    place = jnp.concatenate([jnp.zeros((8,), jnp.int32)] + place).astype(jnp.int32)
    meta = jnp.concatenate([ends, place[8:]])

    target = teacher(place, queries, teacher_pieces)
    student_parts, target = lax.optimization_barrier((student_parts, target))
    student_pieces = with_other_core(student_parts)
    query_grad, here_mine, here_other, near_mine, near_other, far_mine, far_other = student(
        meta, queries, target, student_pieces
    )
    far = far_mine.astype(f32) + swap_cores(far_other).astype(f32)
    far = far.astype(bf16)
    relayed = [chip_shift(far[:HALF], 1), chip_shift(far[HALF:], 3)]
    near = near_mine.astype(f32) + swap_cores(near_other).astype(f32)
    ahead = jnp.concatenate([near[0, :HALF] + relayed[0].astype(f32), near[0, HALF:]]).astype(bf16)
    behind = jnp.concatenate([near[1, :HALF], near[1, HALF:] + relayed[1].astype(f32)]).astype(bf16)
    received = [chip_shift(ahead, 1), chip_shift(behind, 3)]
    total = here_mine.astype(f32) + swap_cores(here_other).astype(f32)
    for part in received:
        total = total + part.astype(f32)
    query_out = unpack_one(exchange(query_grad.reshape(HEADS, SHARD, DH), SETS))
    key_out, value_out = unpack_two(
        exchange_groups(total.astype(bf16).reshape(HEADS, SHARD, 2 * DH))
    )
    return (query_out[None], key_out[None], value_out[None])


def solution(mesh):
    spec = P("blk", "seq", None)
    return jax.shard_map(
        per_device,
        mesh=mesh,
        in_specs=(spec,) * 6 + (P("blk", "seq"),),
        out_specs=(spec,) * 3,
        check_vma=False,
    )
```

```python
import functools

import jax
import jax.numpy as jnp
from jax import lax
from jax.experimental import pallas as pl
from jax.experimental.pallas import tpu as pltpu
from jax.sharding import PartitionSpec as P

DH = 128
HEADS = 32
SHARD = 32
ROWS = 1024
HALF = 512
TOKENS = 8192
EXTRA = 16
MEMBERS = 32
HALF_MEMBERS = 16
scale = DH ** -0.5
scale_log2 = scale * 1.4426950408889634
loss_scale = 64.0
hidden_bias = -131072.0
f32 = jnp.float32
bf16 = jnp.bfloat16
VMEM = pl.BlockSpec(memory_space=pltpu.VMEM)
SMEM = pl.BlockSpec(memory_space=pltpu.SMEM)
ANY = pl.BlockSpec(memory_space=pl.ANY)


def params():
    return pltpu.CompilerParams(vmem_limit_bytes=60 * 2**20)


def dot(a, b):
    return jnp.dot(a, b, preferred_element_type=f32)


def pack_kernel(count, *refs):
    out_ref = refs[-1]
    for h in range(HEADS):
        for n in range(count):
            out_ref[h, n * SHARD:(n + 1) * SHARD, :] = refs[n][:, h * DH:(h + 1) * DH]
        if len(refs) > count + 1:
            out_ref[h, count * SHARD:, :] = refs[count][...]


def pack(arrays, extra=()):
    count = len(arrays)
    rows = count * SHARD + sum(x.shape[0] for x in extra)
    return pl.pallas_call(
        functools.partial(pack_kernel, count),
        out_shape=jax.ShapeDtypeStruct((HEADS, rows, DH), bf16),
        in_specs=[VMEM] * (count + len(extra)),
        out_specs=VMEM,
        compiler_params=params(),
    )(*arrays, *extra)


def unpack_kernel(in_ref, *out_refs):
    for h in range(HEADS):
        for n in range(len(out_refs)):
            out_refs[n][:, h * DH:(h + 1) * DH] = in_ref[h, n * SHARD:(n + 1) * SHARD, :]


def unpack(rows):
    return pl.pallas_call(
        unpack_kernel,
        out_shape=[jax.ShapeDtypeStruct((SHARD, HEADS * DH), bf16)] * (rows.shape[1] // SHARD),
        in_specs=[VMEM],
        out_specs=[VMEM] * (rows.shape[1] // SHARD),
        compiler_params=params(),
    )(rows)


def fold(op, x):
    return op(x.reshape(-1, 8, x.shape[-1]), axis=0)


def online_step(scores, values_t, cols, max_ref, sum_ref, out_ref):
    before = max_ref[0:1, cols]
    highest = jnp.max(fold(jnp.max, scores), axis=0, keepdims=True) * scale_log2
    now = jnp.maximum(before, highest)
    shrink = jnp.exp2(before - now)
    weights = jnp.exp2(scores * scale_log2 - now)
    rounded = weights.astype(bf16)
    block_sum = jnp.sum(fold(jnp.sum, weights), axis=0, keepdims=True)
    sum_ref[0:1, cols] = sum_ref[0:1, cols] * shrink + block_sum
    out_ref[:, cols] = out_ref[:, cols] * shrink + dot(values_t, rounded)
    max_ref[0:1, cols] = now
    return rounded, now


STATE = [(8, ROWS), (8, ROWS), (DH, ROWS)]


def state_shapes():
    return [jax.ShapeDtypeStruct(shape, f32) for shape in STATE]


def open_state(before, after):
    if before:
        for old, new in zip(before, after):
            new[...] = old[...]
    else:
        after[0][...] = jnp.full((8, ROWS), -1e30, f32)
        after[1][...] = jnp.zeros((8, ROWS), f32)
        after[2][...] = jnp.zeros((DH, ROWS), f32)


def members_of(pieces):
    return sum(piece.shape[0] for piece in pieces)


def load_pieces(pieces, held, sems):
    copies, at = [], 0
    for i, piece in enumerate(pieces):
        members = piece.shape[0]
        copies.append(pltpu.make_async_copy(piece, held.at[pl.ds(at, members)], sems.at[i]))
        at += members
    for copy in copies:
        copy.start()
    return copies


def take(own_ref, other_ref, part, meta_ref):
    rows = slice(part * SHARD, (part + 1) * SHARD)
    own = own_ref[:, rows, :].reshape(HALF, DH)
    other = other_ref[:, rows, :].reshape(HALF, DH)
    own_first = meta_ref[10] > 0
    return jnp.concatenate(
        [jnp.where(own_first, own, other), jnp.where(own_first, other, own)], axis=0
    )


def keys_of(held, i, count=1):
    members = pl.ds(pl.multiple_of(i * MEMBERS, MEMBERS), count * MEMBERS)
    return held[members, :SHARD, :].reshape(count * ROWS, DH)


def values_of(held, i, count=1):
    members = pl.ds(pl.multiple_of(i * MEMBERS, MEMBERS), count * MEMBERS)
    return held[members, SHARD:, :].reshape(count * ROWS, DH)


def keys_of(held, i, count=1):
    members = pl.ds(pl.multiple_of(i * MEMBERS, MEMBERS), count * MEMBERS)
    return held[members, :SHARD, :].reshape(count * ROWS, DH)


def values_of(held, i, count=1):
    members = pl.ds(pl.multiple_of(i * MEMBERS, MEMBERS), count * MEMBERS)
    return held[members, SHARD:, :].reshape(count * ROWS, DH)


def rows_of(i):
    return pl.ds(pl.multiple_of(i * ROWS, ROWS), ROWS)


def teacher_kernel(n_before, n_pieces, last, meta_ref, own_ref, other_ref, *rest):
    before, pieces = rest[:n_before], rest[n_before:n_before + n_pieces]
    rest = rest[n_before + n_pieces:]
    if last:
        target_ref, held, sems = rest[:3]
        state = rest[3:]
    else:
        state, held, sems = rest[:3], rest[3], rest[4]
    copies = load_pieces(pieces, held, sems)
    open_state(before, state)
    queries_t = take(own_ref, other_ref, 0, meta_ref).T
    for copy in copies:
        copy.wait()

    def step(i, _):
        keys = keys_of(held, 2 * i, 2)
        values_t = values_of(held, 2 * i, 2).T
        for first in (0, HALF):
            cols = slice(first, first + HALF)
            online_step(dot(keys, queries_t[:, cols]), values_t, cols, *state)
        return 0

    lax.fori_loop(0, held.shape[0] // (2 * MEMBERS), step, 0)
    if last:
        target_ref[...] = (state[2][...] / state[1][0:1, :]).astype(bf16)


def teacher(meta, own, other, state, pieces, last=False):
    members = members_of(pieces)
    held = pltpu.VMEM((members, 2 * SHARD, DH), bf16)
    scratch = [held, pltpu.SemaphoreType.DMA((len(pieces),))]
    if last:
        out_shape = [jax.ShapeDtypeStruct((DH, ROWS), bf16)]
        scratch += [pltpu.VMEM(shape, f32) for shape in STATE]
    else:
        out_shape = state_shapes()
    return pl.pallas_call(
        functools.partial(teacher_kernel, len(state), len(pieces), last),
        out_shape=out_shape,
        in_specs=[SMEM, VMEM, VMEM] + [VMEM] * len(state) + [ANY] * len(pieces),
        out_specs=[VMEM] * len(out_shape),
        scratch_shapes=scratch,
        compiler_params=params(),
        cost_estimate=pl.CostEstimate(
            flops=members * 6 * 10**7, bytes_accessed=members * 2**14, transcendentals=0
        ),
    )(meta, own, other, *state, *pieces)


def frames_of(tokens, meta_ref):
    frames = jnp.zeros(tokens.shape, jnp.int32)
    for f in range(6):
        frames = frames + (tokens >= meta_ref[f]).astype(jnp.int32)
    return frames


def groups_seen(meta_ref, last):
    seen = jnp.int32(TOKENS)
    for f in range(6, -1, -1):
        seen = jnp.where(last < meta_ref[f], meta_ref[f], seen)
    return (seen + (ROWS - 1)) // ROWS


def keys_with_frames(keys, group, meta_ref):
    column = lax.broadcasted_iota(jnp.int32, (ROWS, DH), 1)
    tokens = group * ROWS + lax.broadcasted_iota(jnp.int32, (ROWS, DH), 0)
    one_hot = (frames_of(tokens, meta_ref) == column).astype(f32).astype(bf16)
    return jnp.concatenate([keys, one_hot], axis=1)


def by_visibility(meta_ref, group, compute, skip=None):
    seen_early = groups_seen(meta_ref, meta_ref[8] + (HALF - 1))
    seen_late = groups_seen(meta_ref, meta_ref[9] + (HALF - 1))

    @pl.when(group < seen_early)
    def _():
        compute(0)

    @pl.when((group >= seen_early) & (group < seen_late))
    def _():
        compute(HALF)

    if skip is not None:

        @pl.when(group >= seen_late)
        def _():
            skip()


def student_kernel(meta_ref, own_ref, other_ref, target_ref, *rest):
    pieces = rest[:10]
    dq_own_ref, dq_other_ref = rest[10:12]
    outs = rest[12:18]
    held, max_ref, sum_ref, out_ref, weights_ref, max_at, dqt, qt_ref, kv_grad = rest[18:27]
    sems, out_sems = rest[27:]
    copies = load_pieces(pieces, held, sems)
    open_state((), (max_ref, sum_ref, out_ref))
    dqt[...] = jnp.zeros(dqt.shape, f32)
    queries = take(own_ref, other_ref, 1, meta_ref)
    column = lax.broadcasted_iota(jnp.int32, (DH, ROWS), 1)
    row = lax.broadcasted_iota(jnp.int32, (DH, ROWS), 0)
    tokens = jnp.where(column < HALF, meta_ref[8] + column, meta_ref[9] + (column - HALF))
    bias = jnp.where((row > frames_of(tokens, meta_ref)) & (row < 7), hidden_bias, 0.0)
    qt_ref[:DH, :] = queries.T
    qt_ref[DH:, :] = bias.astype(bf16)
    for copy in copies:
        copy.wait()

    def forward(i, _):
        group = meta_ref[16 + i]

        def compute(first):
            rows, cols = rows_of(i), slice(first, ROWS)
            keys = keys_with_frames(keys_of(held, i), group, meta_ref)
            rounded, now = online_step(
                dot(keys, qt_ref[:, cols]), values_of(held, i).T, cols, max_ref, sum_ref, out_ref
            )
            weights_ref[rows, cols] = rounded
            at = pl.ds(pl.multiple_of(i * 8, 8), 8)
            max_at[at, cols] = jnp.broadcast_to(now, (8, ROWS - first))

        by_visibility(meta_ref, group, compute)
        return 0

    lax.fori_loop(0, 8, forward, 0)

    inverse = 1.0 / sum_ref[0:1, :]
    output = out_ref[...] * inverse
    out_grad = (loss_scale * (output - target_ref[...].astype(f32))).astype(bf16).astype(f32)
    delta = jnp.sum(out_grad * output, axis=0, keepdims=True) * inverse
    grad_t = (out_grad * inverse).astype(bf16)
    delta_1 = delta.astype(bf16).astype(f32)
    delta_2 = (delta - delta_1).astype(bf16).astype(f32)
    delta_3 = delta - delta_1 - delta_2
    delta_rows = jnp.where(
        row == 0, -delta_1, jnp.where(row == 1, -delta_2, jnp.where(row == 2, -delta_3, 0.0))
    )
    grad_delta_t = jnp.concatenate([grad_t, delta_rows.astype(bf16)], axis=0)
    grad = grad_t.T
    key_column = lax.broadcasted_iota(jnp.int32, (ROWS, DH), 1)
    ones = jnp.where(key_column < 3, 1.0, 0.0).astype(bf16)

    def backward(i, _):
        group = meta_ref[16 + i]

        def compute(first):
            rows, cols = rows_of(i), slice(first, ROWS)
            values = jnp.concatenate([values_of(held, i), ones], axis=1)
            centred = dot(values, grad_delta_t[:, cols])
            at = pl.ds(pl.multiple_of(i * 8, 8), 8)
            shrink = jnp.exp2(max_at[at, cols][0:1] - max_ref[0:1, cols])
            weights = weights_ref[rows, cols].astype(f32) * shrink
            score_grad = (weights * centred).astype(bf16)
            members = pl.ds(pl.multiple_of(i * MEMBERS, MEMBERS), MEMBERS)
            value_grad = dot(weights.astype(bf16), grad[cols])
            key_grad = dot(score_grad, queries[cols]) * scale
            kv_grad[members, SHARD:, :] = value_grad.astype(bf16).reshape(MEMBERS, SHARD, DH)
            kv_grad[members, :SHARD, :] = key_grad.astype(bf16).reshape(MEMBERS, SHARD, DH)
            dqt[:, cols] += dot(keys_of(held, i).T, score_grad)

        def skip():
            members = pl.ds(pl.multiple_of(i * MEMBERS, MEMBERS), MEMBERS)
            kv_grad[members, :, :] = jnp.zeros((MEMBERS, 2 * SHARD, DH), bf16)

        by_visibility(meta_ref, group, compute, skip)
        return 0

    lax.fori_loop(0, 8, backward, 0)
    out_copies = [
        pltpu.make_async_copy(kv_grad.at[pl.ds(i * MEMBERS, MEMBERS)], out, out_sems.at[k])
        for k, (i, out) in enumerate(
            [(0, outs[0]), (1, outs[1]), (2, outs[2].at[0]), (4, outs[2].at[1])]
            + [(3, outs[3].at[0]), (5, outs[3].at[1]), (6, outs[4]), (7, outs[5])]
        )
    ]
    for copy in out_copies:
        copy.start()
    query_grad = (dqt[...] * scale).T.astype(bf16)
    own_first = meta_ref[10] > 0
    first, second = query_grad[:HALF], query_grad[HALF:]
    shape = (HALF_MEMBERS, SHARD, DH)
    dq_own_ref[...] = jnp.where(own_first, first, second).reshape(shape)
    dq_other_ref[...] = jnp.where(own_first, second, first).reshape(shape)
    for copy in out_copies:
        copy.wait()


def student(meta, own, other, target, pieces):
    half = jax.ShapeDtypeStruct((HALF_MEMBERS, SHARD, DH), bf16)
    one = jax.ShapeDtypeStruct((MEMBERS, 2 * SHARD, DH), bf16)
    two = jax.ShapeDtypeStruct((2, MEMBERS, 2 * SHARD, DH), bf16)
    return pl.pallas_call(
        student_kernel,
        out_shape=[half, half, one, one, two, two, one, one],
        in_specs=[SMEM, VMEM, VMEM, VMEM] + [ANY] * 10,
        out_specs=[VMEM] * 2 + [ANY] * 6,
        scratch_shapes=[
            pltpu.VMEM((8 * MEMBERS, 2 * SHARD, DH), bf16),
            pltpu.VMEM((8, ROWS), f32),
            pltpu.VMEM((8, ROWS), f32),
            pltpu.VMEM((DH, ROWS), f32),
            pltpu.VMEM((TOKENS, ROWS), bf16),
            pltpu.VMEM((64, ROWS), f32),
            pltpu.VMEM((DH, ROWS), f32),
            pltpu.VMEM((2 * DH, ROWS), bf16),
            pltpu.VMEM((8 * MEMBERS, 2 * SHARD, DH), bf16),
            pltpu.SemaphoreType.DMA((10,)),
            pltpu.SemaphoreType.DMA((8,)),
        ],
        compiler_params=params(),
        cost_estimate=pl.CostEstimate(
            flops=26 * 10**9, bytes_accessed=10 * 2**20, transcendentals=ROWS * TOKENS
        ),
    )(meta, own, other, target, *pieces)


def exchange(packed):
    return lax.all_to_all(packed, "seq", split_axis=0, concat_axis=0, tiled=True)


def trade(x):
    return lax.ppermute(x, "blk", [(i, 7 - i) for i in range(8)])


def chip_shift(x, by):
    return lax.ppermute(x, "blk", [(i, ((i // 2 + by) % 4) * 2 + i % 2) for i in range(8)])


def swap_cores(x):
    return lax.ppermute(x, "blk", [(i, i ^ 1) for i in range(8)])


def with_other_core(parts):
    return [x for part in parts for x in (part, swap_cores(part))]


def frame_ends(counted):
    counts = jnp.broadcast_to(jnp.sum(counted.astype(f32), axis=0)[:, None], (8, DH))
    counts = counts + swap_cores(counts)
    counts = counts + chip_shift(counts, 1)
    counts = counts + chip_shift(counts, 2)
    return counts[:, 0].astype(jnp.int32)


def per_device(
    teacher_query,
    teacher_key,
    teacher_value,
    student_query,
    student_key,
    student_value,
    frame_index,
):
    blk = lax.axis_index("blk")
    seq = lax.axis_index("seq")
    frame_ids = jnp.arange(DH, dtype=jnp.int32)
    counts = jnp.sum((frame_index[0][:, None] <= frame_ids[None, :]).astype(f32), axis=0)
    counts = jnp.broadcast_to(counts.astype(bf16), (EXTRA, DH))
    tie = lax.optimization_barrier
    arrays = (teacher_key, teacher_value, teacher_query, student_query)
    moved = exchange(pack([x[0] for x in arrays], (counts,)))
    student_key, student_value, moved = tie((student_key, student_value, moved))
    student_kv = exchange(pack([student_key[0], student_value[0]]))
    teacher_kv = moved[:, :2 * SHARD]
    early = seq < HALF_MEMBERS
    keep = jnp.where(early, 0, HALF_MEMBERS)

    def half_of(x, at):
        return lax.dynamic_slice_in_dim(x, at, HALF_MEMBERS, axis=0)

    queries = moved[:, 2 * SHARD:4 * SHARD]
    own = half_of(queries, keep)
    other = trade(half_of(queries, HALF_MEMBERS - keep))

    chip, core = blk // 2, blk % 2
    own_start = blk * ROWS + jnp.where(early, 0, HALF)
    other_start = (7 - blk) * ROWS + jnp.where(early, HALF, 0)
    halves = jnp.stack([jnp.minimum(own_start, other_start), jnp.maximum(own_start, other_start)])
    groups = []
    for by in (0, 1, 3, 2):
        groups += [((chip + by) % 4) * 2 + core, ((chip + by) % 4) * 2 + 1 - core]
    own_first = (own_start < other_start).astype(jnp.int32)
    place = [halves, own_first[None], jnp.zeros((5,), jnp.int32), jnp.stack(groups)]
    place = jnp.concatenate([jnp.zeros((8,), jnp.int32)] + place).astype(jnp.int32)

    def near_pieces(after, before):
        return with_other_core([after, before])

    def far_halves(before, after):
        return [chip_shift(before[:HALF_MEMBERS], 1), chip_shift(after[HALF_MEMBERS:], 3)]

    teacher_after, teacher_before = chip_shift(teacher_kv, 3), chip_shift(teacher_kv, 1)
    student_after, student_before = chip_shift(student_kv, 3), chip_shift(student_kv, 1)
    ends = frame_ends(moved[:, 4 * SHARD, :8])
    meta = jnp.concatenate([ends, place[8:]])
    teacher_here = with_other_core([teacher_kv])
    teacher_near = near_pieces(teacher_after, teacher_before)
    teacher_far = far_halves(teacher_before, teacher_after)
    teacher_far, own = tie((teacher_far, own))
    teacher_far += [swap_cores(x) for x in teacher_far]
    student_here = with_other_core([student_kv])
    student_near = near_pieces(student_after, student_before)

    taught = teacher(place, own, other, [], teacher_here + teacher_near)
    taught, student_before, student_after = tie((taught, student_before, student_after))
    student_halves = far_halves(student_before, student_after)
    (target,) = teacher(place, own, other, taught, teacher_far, last=True)
    target, student_halves = tie((target, student_halves))
    student_far = student_halves + [swap_cores(x) for x in student_halves]
    grads = student(meta, own, other, target, student_here + student_near + student_far)
    query_own, query_other, here_mine, here_other, near_mine, near_other, far_mine, far_other = grads
    far = (far_mine.astype(f32) + swap_cores(far_other).astype(f32)).astype(bf16)
    query_back = trade(query_other)
    by_ahead = chip_shift(far[:HALF_MEMBERS], 1).astype(f32)
    by_behind = chip_shift(far[HALF_MEMBERS:], 3).astype(f32)
    near = near_mine.astype(f32) + swap_cores(near_other).astype(f32)
    ahead = jnp.concatenate([near[0, :HALF_MEMBERS] + by_ahead, near[0, HALF_MEMBERS:]])
    behind = jnp.concatenate([near[1, :HALF_MEMBERS], near[1, HALF_MEMBERS:] + by_behind])
    total = here_mine.astype(f32) + swap_cores(here_other).astype(f32)
    for part in (chip_shift(ahead.astype(bf16), 1), chip_shift(behind.astype(bf16), 3)):
        total = total + part.astype(f32)
    query_grad = jnp.concatenate(
        [jnp.where(early, query_own, query_back), jnp.where(early, query_back, query_own)]
    )
    (query_out,) = unpack(exchange(query_grad))
    key_out, value_out = unpack(exchange(total.astype(bf16)))
    return (query_out[None], key_out[None], value_out[None])


def solution(mesh):
    spec = P("blk", "seq", None)
    return jax.shard_map(
        per_device,
        mesh=mesh,
        in_specs=(spec,) * 6 + (P("blk", "seq"),),
        out_specs=(spec,) * 3,
        check_vma=False,
    )
```

```python
import functools

import jax
import jax.numpy as jnp
from jax import lax
from jax.experimental import pallas as pl
from jax.experimental.pallas import tpu as pltpu
from jax.sharding import PartitionSpec as P

DH = 128
HEADS = 32
SHARD = 32
ROWS = 1024
HALF = 512
TOKENS = 8192
EXTRA = 16
MEMBERS = 32
HALF_MEMBERS = 16
scale = DH ** -0.5
scale_log2 = scale * 1.4426950408889634
loss_scale = 64.0
hidden_bias = -131072.0
f32 = jnp.float32
bf16 = jnp.bfloat16
VMEM = pl.BlockSpec(memory_space=pltpu.VMEM)
SMEM = pl.BlockSpec(memory_space=pltpu.SMEM)
ANY = pl.BlockSpec(memory_space=pl.ANY)


def params():
    return pltpu.CompilerParams(vmem_limit_bytes=60 * 2**20)


def dot(a, b):
    return jnp.dot(a, b, preferred_element_type=f32)


def pack_kernel(count, *refs):
    out_ref = refs[-1]
    for h in range(HEADS):
        for n in range(count):
            out_ref[h, n * SHARD:(n + 1) * SHARD, :] = refs[n][:, h * DH:(h + 1) * DH]
        if len(refs) > count + 1:
            out_ref[h, count * SHARD:, :] = refs[count][...]


def pack(arrays, extra=()):
    count = len(arrays)
    rows = count * SHARD + sum(x.shape[0] for x in extra)
    return pl.pallas_call(
        functools.partial(pack_kernel, count),
        out_shape=jax.ShapeDtypeStruct((HEADS, rows, DH), bf16),
        in_specs=[VMEM] * (count + len(extra)),
        out_specs=VMEM,
        compiler_params=params(),
    )(*arrays, *extra)


def unpack_kernel(in_ref, *out_refs):
    for h in range(HEADS):
        for n in range(len(out_refs)):
            out_refs[n][:, h * DH:(h + 1) * DH] = in_ref[h, n * SHARD:(n + 1) * SHARD, :]


def unpack(rows):
    return pl.pallas_call(
        unpack_kernel,
        out_shape=[jax.ShapeDtypeStruct((SHARD, HEADS * DH), bf16)] * (rows.shape[1] // SHARD),
        in_specs=[VMEM],
        out_specs=[VMEM] * (rows.shape[1] // SHARD),
        compiler_params=params(),
    )(rows)


def fold(op, x):
    return op(x.reshape(-1, 8, x.shape[-1]), axis=0)


def online_step(scores, values_t, cols, max_ref, sum_ref, out_ref):
    before = max_ref[0:1, cols]
    highest = jnp.max(fold(jnp.max, scores), axis=0, keepdims=True) * scale_log2
    now = jnp.maximum(before, highest)
    shrink = jnp.exp2(before - now)
    weights = jnp.exp2(scores * scale_log2 - now)
    rounded = weights.astype(bf16)
    block_sum = jnp.sum(fold(jnp.sum, weights), axis=0, keepdims=True)
    sum_ref[0:1, cols] = sum_ref[0:1, cols] * shrink + block_sum
    out_ref[:, cols] = out_ref[:, cols] * shrink + dot(values_t, rounded)
    max_ref[0:1, cols] = now
    return rounded, now


STATE = [(8, ROWS), (8, ROWS), (DH, ROWS)]


def state_shapes():
    return [jax.ShapeDtypeStruct(shape, f32) for shape in STATE]


def open_state(before, after):
    if before:
        for old, new in zip(before, after):
            new[...] = old[...]
    else:
        after[0][...] = jnp.full((8, ROWS), -1e30, f32)
        after[1][...] = jnp.zeros((8, ROWS), f32)
        after[2][...] = jnp.zeros((DH, ROWS), f32)


def members_of(pieces):
    return sum(piece.shape[0] for piece in pieces)


def load_pieces(pieces, held, sems):
    copies, at = [], 0
    for i, piece in enumerate(pieces):
        members = piece.shape[0]
        copies.append(pltpu.make_async_copy(piece, held.at[pl.ds(at, members)], sems.at[i]))
        at += members
    for copy in copies:
        copy.start()
    return copies


def take(own_ref, other_ref, part, meta_ref):
    rows = slice(part * SHARD, (part + 1) * SHARD)
    own = own_ref[:, rows, :].reshape(HALF, DH)
    other = other_ref[:, rows, :].reshape(HALF, DH)
    own_first = meta_ref[10] > 0
    return jnp.concatenate(
        [jnp.where(own_first, own, other), jnp.where(own_first, other, own)], axis=0
    )


def keys_of(held, i, count=1):
    members = pl.ds(pl.multiple_of(i * MEMBERS, MEMBERS), count * MEMBERS)
    return held[members, :SHARD, :].reshape(count * ROWS, DH)


def values_of(held, i, count=1):
    members = pl.ds(pl.multiple_of(i * MEMBERS, MEMBERS), count * MEMBERS)
    return held[members, SHARD:, :].reshape(count * ROWS, DH)


def keys_of(held, i, count=1):
    members = pl.ds(pl.multiple_of(i * MEMBERS, MEMBERS), count * MEMBERS)
    return held[members, :SHARD, :].reshape(count * ROWS, DH)


def values_of(held, i, count=1):
    members = pl.ds(pl.multiple_of(i * MEMBERS, MEMBERS), count * MEMBERS)
    return held[members, SHARD:, :].reshape(count * ROWS, DH)


def rows_of(i):
    return pl.ds(pl.multiple_of(i * ROWS, ROWS), ROWS)


def teacher_kernel(n_before, n_pieces, last, meta_ref, own_ref, other_ref, *rest):
    before, pieces = rest[:n_before], rest[n_before:n_before + n_pieces]
    rest = rest[n_before + n_pieces:]
    if last:
        target_ref, held, sems = rest[:3]
        state = rest[3:]
    else:
        state, held, sems = rest[:3], rest[3], rest[4]
    copies = load_pieces(pieces, held, sems)
    open_state(before, state)
    queries_t = take(own_ref, other_ref, 0, meta_ref).T
    for copy in copies:
        copy.wait()

    def step(i, _):
        keys = keys_of(held, 2 * i, 2)
        values_t = values_of(held, 2 * i, 2).T
        for first in (0, HALF):
            cols = slice(first, first + HALF)
            online_step(dot(keys, queries_t[:, cols]), values_t, cols, *state)
        return 0

    lax.fori_loop(0, held.shape[0] // (2 * MEMBERS), step, 0)
    if last:
        target_ref[...] = (state[2][...] / state[1][0:1, :]).astype(bf16)


def teacher(meta, own, other, state, pieces, last=False):
    members = members_of(pieces)
    held = pltpu.VMEM((members, 2 * SHARD, DH), bf16)
    scratch = [held, pltpu.SemaphoreType.DMA((len(pieces),))]
    if last:
        out_shape = [jax.ShapeDtypeStruct((DH, ROWS), bf16)]
        scratch += [pltpu.VMEM(shape, f32) for shape in STATE]
    else:
        out_shape = state_shapes()
    return pl.pallas_call(
        functools.partial(teacher_kernel, len(state), len(pieces), last),
        out_shape=out_shape,
        in_specs=[SMEM, VMEM, VMEM] + [VMEM] * len(state) + [ANY] * len(pieces),
        out_specs=[VMEM] * len(out_shape),
        scratch_shapes=scratch,
        compiler_params=params(),
        cost_estimate=pl.CostEstimate(
            flops=members * 6 * 10**7, bytes_accessed=members * 2**14, transcendentals=0
        ),
    )(meta, own, other, *state, *pieces)


def frames_of(tokens, meta_ref):
    frames = jnp.zeros(tokens.shape, jnp.int32)
    for f in range(6):
        frames = frames + (tokens >= meta_ref[f]).astype(jnp.int32)
    return frames


def groups_seen(meta_ref, last):
    seen = jnp.int32(TOKENS)
    for f in range(6, -1, -1):
        seen = jnp.where(last < meta_ref[f], meta_ref[f], seen)
    return (seen + (ROWS - 1)) // ROWS


def keys_with_frames(keys, group, meta_ref):
    column = lax.broadcasted_iota(jnp.int32, (ROWS, DH), 1)
    tokens = group * ROWS + lax.broadcasted_iota(jnp.int32, (ROWS, DH), 0)
    one_hot = (frames_of(tokens, meta_ref) == column).astype(f32).astype(bf16)
    return jnp.concatenate([keys, one_hot], axis=1)


def by_visibility(meta_ref, group, compute, skip=None):
    seen_early = groups_seen(meta_ref, meta_ref[8] + (HALF - 1))
    seen_late = groups_seen(meta_ref, meta_ref[9] + (HALF - 1))

    @pl.when(group < seen_early)
    def _():
        compute(0)

    @pl.when((group >= seen_early) & (group < seen_late))
    def _():
        compute(HALF)

    if skip is not None:

        @pl.when(group >= seen_late)
        def _():
            skip()


def student_kernel(meta_ref, own_ref, other_ref, target_ref, *rest):
    pieces = rest[:10]
    dq_own_ref, dq_other_ref = rest[10:12]
    outs = rest[12:18]
    held, max_ref, sum_ref, out_ref, weights_ref, max_at, dqt, qt_ref, kv_grad = rest[18:27]
    sems, out_sems = rest[27:]
    copies = load_pieces(pieces, held, sems)
    open_state((), (max_ref, sum_ref, out_ref))
    dqt[...] = jnp.zeros(dqt.shape, f32)
    queries = take(own_ref, other_ref, 1, meta_ref)
    column = lax.broadcasted_iota(jnp.int32, (DH, ROWS), 1)
    row = lax.broadcasted_iota(jnp.int32, (DH, ROWS), 0)
    tokens = jnp.where(column < HALF, meta_ref[8] + column, meta_ref[9] + (column - HALF))
    bias = jnp.where((row > frames_of(tokens, meta_ref)) & (row < 7), hidden_bias, 0.0)
    qt_ref[:DH, :] = queries.T
    qt_ref[DH:, :] = bias.astype(bf16)
    for copy in copies:
        copy.wait()

    def forward(i, _):
        group = meta_ref[16 + i]

        def compute(first):
            rows, cols = rows_of(i), slice(first, ROWS)
            keys = keys_with_frames(keys_of(held, i), group, meta_ref)
            rounded, now = online_step(
                dot(keys, qt_ref[:, cols]), values_of(held, i).T, cols, max_ref, sum_ref, out_ref
            )
            weights_ref[rows, cols] = rounded
            at = pl.ds(pl.multiple_of(i * 8, 8), 8)
            max_at[at, cols] = jnp.broadcast_to(now, (8, ROWS - first))

        by_visibility(meta_ref, group, compute)
        return 0

    lax.fori_loop(0, 8, forward, 0)

    inverse = 1.0 / sum_ref[0:1, :]
    output = out_ref[...] * inverse
    out_grad = (loss_scale * (output - target_ref[...].astype(f32))).astype(bf16).astype(f32)
    delta = jnp.sum(out_grad * output, axis=0, keepdims=True) * inverse
    grad_t = (out_grad * inverse).astype(bf16)
    delta_1 = delta.astype(bf16).astype(f32)
    delta_2 = (delta - delta_1).astype(bf16).astype(f32)
    delta_3 = delta - delta_1 - delta_2
    delta_rows = jnp.where(
        row == 0, -delta_1, jnp.where(row == 1, -delta_2, jnp.where(row == 2, -delta_3, 0.0))
    )
    grad_delta_t = jnp.concatenate([grad_t, delta_rows.astype(bf16)], axis=0)
    grad = grad_t.T
    key_column = lax.broadcasted_iota(jnp.int32, (ROWS, DH), 1)
    ones = jnp.where(key_column < 3, 1.0, 0.0).astype(bf16)

    def backward(i, _):
        group = meta_ref[16 + i]

        def compute(first):
            rows, cols = rows_of(i), slice(first, ROWS)
            values = jnp.concatenate([values_of(held, i), ones], axis=1)
            centred = dot(values, grad_delta_t[:, cols])
            at = pl.ds(pl.multiple_of(i * 8, 8), 8)
            shrink = jnp.exp2(max_at[at, cols][0:1] - max_ref[0:1, cols])
            weights = weights_ref[rows, cols].astype(f32) * shrink
            score_grad = (weights * centred).astype(bf16)
            members = pl.ds(pl.multiple_of(i * MEMBERS, MEMBERS), MEMBERS)
            value_grad = dot(weights.astype(bf16), grad[cols])
            key_grad = dot(score_grad, queries[cols]) * scale
            kv_grad[members, SHARD:, :] = value_grad.astype(bf16).reshape(MEMBERS, SHARD, DH)
            kv_grad[members, :SHARD, :] = key_grad.astype(bf16).reshape(MEMBERS, SHARD, DH)
            dqt[:, cols] += dot(keys_of(held, i).T, score_grad)

        def skip():
            members = pl.ds(pl.multiple_of(i * MEMBERS, MEMBERS), MEMBERS)
            kv_grad[members, :, :] = jnp.zeros((MEMBERS, 2 * SHARD, DH), bf16)

        by_visibility(meta_ref, group, compute, skip)
        return 0

    lax.fori_loop(0, 8, backward, 0)
    out_copies = [
        pltpu.make_async_copy(kv_grad.at[pl.ds(i * MEMBERS, MEMBERS)], out, out_sems.at[k])
        for k, (i, out) in enumerate(
            [(0, outs[0]), (1, outs[1]), (2, outs[2].at[0]), (4, outs[2].at[1])]
            + [(3, outs[3].at[0]), (5, outs[3].at[1]), (6, outs[4]), (7, outs[5])]
        )
    ]
    for copy in out_copies:
        copy.start()
    query_grad = (dqt[...] * scale).T.astype(bf16)
    own_first = meta_ref[10] > 0
    first, second = query_grad[:HALF], query_grad[HALF:]
    shape = (HALF_MEMBERS, SHARD, DH)
    dq_own_ref[...] = jnp.where(own_first, first, second).reshape(shape)
    dq_other_ref[...] = jnp.where(own_first, second, first).reshape(shape)
    for copy in out_copies:
        copy.wait()


def student(meta, own, other, target, pieces):
    half = jax.ShapeDtypeStruct((HALF_MEMBERS, SHARD, DH), bf16)
    one = jax.ShapeDtypeStruct((MEMBERS, 2 * SHARD, DH), bf16)
    two = jax.ShapeDtypeStruct((2, MEMBERS, 2 * SHARD, DH), bf16)
    return pl.pallas_call(
        student_kernel,
        out_shape=[half, half, one, one, two, two, one, one],
        in_specs=[SMEM, VMEM, VMEM, VMEM] + [ANY] * 10,
        out_specs=[VMEM] * 2 + [ANY] * 6,
        scratch_shapes=[
            pltpu.VMEM((8 * MEMBERS, 2 * SHARD, DH), bf16),
            pltpu.VMEM((8, ROWS), f32),
            pltpu.VMEM((8, ROWS), f32),
            pltpu.VMEM((DH, ROWS), f32),
            pltpu.VMEM((TOKENS, ROWS), bf16),
            pltpu.VMEM((64, ROWS), f32),
            pltpu.VMEM((DH, ROWS), f32),
            pltpu.VMEM((2 * DH, ROWS), bf16),
            pltpu.VMEM((8 * MEMBERS, 2 * SHARD, DH), bf16),
            pltpu.SemaphoreType.DMA((10,)),
            pltpu.SemaphoreType.DMA((8,)),
        ],
        compiler_params=params(),
        cost_estimate=pl.CostEstimate(
            flops=26 * 10**9, bytes_accessed=10 * 2**20, transcendentals=ROWS * TOKENS
        ),
    )(meta, own, other, target, *pieces)


def exchange(packed):
    return lax.all_to_all(packed, "seq", split_axis=0, concat_axis=0, tiled=True)


def trade(x):
    return lax.ppermute(x, "blk", [(i, 7 - i) for i in range(8)])


def chip_shift(x, by):
    return lax.ppermute(x, "blk", [(i, ((i // 2 + by) % 4) * 2 + i % 2) for i in range(8)])


def swap_cores(x):
    return lax.ppermute(x, "blk", [(i, i ^ 1) for i in range(8)])


def with_other_core(parts):
    return [x for part in parts for x in (part, swap_cores(part))]


def frame_ends(counted):
    counts = jnp.broadcast_to(jnp.sum(counted.astype(f32), axis=0)[:, None], (8, DH))
    counts = counts + swap_cores(counts)
    counts = counts + chip_shift(counts, 1)
    counts = counts + chip_shift(counts, 2)
    return counts[:, 0].astype(jnp.int32)


def per_device(
    teacher_query,
    teacher_key,
    teacher_value,
    student_query,
    student_key,
    student_value,
    frame_index,
):
    blk = lax.axis_index("blk")
    seq = lax.axis_index("seq")
    frame_ids = jnp.arange(DH, dtype=jnp.int32)
    counts = jnp.sum((frame_index[0][:, None] <= frame_ids[None, :]).astype(f32), axis=0)
    counts = jnp.broadcast_to(counts.astype(bf16), (EXTRA, DH))
    tie = lax.optimization_barrier
    arrays = (teacher_key, teacher_value, teacher_query, student_query)
    moved = exchange(pack([x[0] for x in arrays], (counts,)))
    student_key, student_value, moved = tie((student_key, student_value, moved))
    student_kv = exchange(pack([student_key[0], student_value[0]]))
    teacher_kv = moved[:, :2 * SHARD]
    early = seq < HALF_MEMBERS
    keep = jnp.where(early, 0, HALF_MEMBERS)

    def half_of(x, at):
        return lax.dynamic_slice_in_dim(x, at, HALF_MEMBERS, axis=0)

    queries = moved[:, 2 * SHARD:4 * SHARD]
    own = half_of(queries, keep)
    other = trade(half_of(queries, HALF_MEMBERS - keep))

    chip, core = blk // 2, blk % 2
    own_start = blk * ROWS + jnp.where(early, 0, HALF)
    other_start = (7 - blk) * ROWS + jnp.where(early, HALF, 0)
    halves = jnp.stack([jnp.minimum(own_start, other_start), jnp.maximum(own_start, other_start)])
    groups = []
    for by in (0, 1, 3, 2):
        groups += [((chip + by) % 4) * 2 + core, ((chip + by) % 4) * 2 + 1 - core]
    own_first = (own_start < other_start).astype(jnp.int32)
    place = [halves, own_first[None], jnp.zeros((5,), jnp.int32), jnp.stack(groups)]
    place = jnp.concatenate([jnp.zeros((8,), jnp.int32)] + place).astype(jnp.int32)

    def near_pieces(after, before):
        return with_other_core([after, before])

    def far_halves(before, after):
        return [chip_shift(before[:HALF_MEMBERS], 1), chip_shift(after[HALF_MEMBERS:], 3)]

    teacher_after, teacher_before = chip_shift(teacher_kv, 3), chip_shift(teacher_kv, 1)
    student_after, student_before = chip_shift(student_kv, 3), chip_shift(student_kv, 1)
    ends = frame_ends(moved[:, 4 * SHARD, :8])
    meta = jnp.concatenate([ends, place[8:]])
    teacher_here = with_other_core([teacher_kv])
    teacher_near = near_pieces(teacher_after, teacher_before)
    teacher_far = far_halves(teacher_before, teacher_after)
    teacher_far += [swap_cores(x) for x in teacher_far]
    student_here = with_other_core([student_kv])
    student_near = near_pieces(student_after, student_before)

    (target,) = teacher(
        place, own, other, [], teacher_here + teacher_near + teacher_far, last=True
    )
    student_before, student_after, target = tie((student_before, student_after, target))
    student_halves = far_halves(student_before, student_after)
    student_far = student_halves + [swap_cores(x) for x in student_halves]
    grads = student(meta, own, other, target, student_here + student_near + student_far)
    query_own, query_other, here_mine, here_other, near_mine, near_other, far_mine, far_other = grads
    far = (far_mine.astype(f32) + swap_cores(far_other).astype(f32)).astype(bf16)
    query_back = trade(query_other)
    by_ahead = chip_shift(far[:HALF_MEMBERS], 1).astype(f32)
    by_behind = chip_shift(far[HALF_MEMBERS:], 3).astype(f32)
    near = near_mine.astype(f32) + swap_cores(near_other).astype(f32)
    ahead = jnp.concatenate([near[0, :HALF_MEMBERS] + by_ahead, near[0, HALF_MEMBERS:]])
    behind = jnp.concatenate([near[1, :HALF_MEMBERS], near[1, HALF_MEMBERS:] + by_behind])
    total = here_mine.astype(f32) + swap_cores(here_other).astype(f32)
    for part in (chip_shift(ahead.astype(bf16), 1), chip_shift(behind.astype(bf16), 3)):
        total = total + part.astype(f32)
    query_grad = jnp.concatenate(
        [jnp.where(early, query_own, query_back), jnp.where(early, query_back, query_own)]
    )
    (query_out,) = unpack(exchange(query_grad))
    key_out, value_out = unpack(exchange(total.astype(bf16)))
    return (query_out[None], key_out[None], value_out[None])


def solution(mesh):
    spec = P("blk", "seq", None)
    return jax.shard_map(
        per_device,
        mesh=mesh,
        in_specs=(spec,) * 6 + (P("blk", "seq"),),
        out_specs=(spec,) * 3,
        check_vma=False,
    )
```

```python
import functools

import jax
import jax.numpy as jnp
from jax import lax
from jax.experimental import pallas as pl
from jax.experimental.pallas import tpu as pltpu
from jax.sharding import PartitionSpec as P

DH = 128
HEADS = 32
SHARD = 32
ROWS = 1024
HALF = 512
TOKENS = 8192
EXTRA = 16
MEMBERS = 32
HALF_MEMBERS = 16
scale = DH ** -0.5
scale_log2 = scale * 1.4426950408889634
loss_scale = 64.0
hidden_bias = -131072.0
f32 = jnp.float32
bf16 = jnp.bfloat16
VMEM = pl.BlockSpec(memory_space=pltpu.VMEM)
SMEM = pl.BlockSpec(memory_space=pltpu.SMEM)
ANY = pl.BlockSpec(memory_space=pl.ANY)


def params():
    return pltpu.CompilerParams(vmem_limit_bytes=60 * 2**20)


def dot(a, b):
    return jnp.dot(a, b, preferred_element_type=f32)


def pack_kernel(count, with_frames, *refs):
    out_ref = refs[-1]
    for h in range(HEADS):
        for n in range(count):
            out_ref[h, n * SHARD:(n + 1) * SHARD, :] = refs[n][:, h * DH:(h + 1) * DH]
    if with_frames:
        column = lax.broadcasted_iota(jnp.int32, (EXTRA, DH), 1)
        counts = jnp.zeros((EXTRA, DH), jnp.int32)
        for k in range(SHARD):
            counts = counts + (refs[count][0, k] <= column).astype(jnp.int32)
        counts = counts.astype(f32).astype(bf16)
        for h in range(HEADS):
            out_ref[h, count * SHARD:, :] = counts


def pack(arrays, frames=()):
    count = len(arrays)
    rows = count * SHARD + EXTRA * len(frames)
    return pl.pallas_call(
        functools.partial(pack_kernel, count, len(frames) > 0),
        out_shape=jax.ShapeDtypeStruct((HEADS, rows, DH), bf16),
        in_specs=[VMEM] * count + [SMEM] * len(frames),
        out_specs=VMEM,
        compiler_params=params(),
    )(*arrays, *frames)


def unpack_kernel(in_ref, *out_refs):
    for h in range(HEADS):
        for n in range(len(out_refs)):
            out_refs[n][:, h * DH:(h + 1) * DH] = in_ref[h, n * SHARD:(n + 1) * SHARD, :]


def unpack(rows):
    return pl.pallas_call(
        unpack_kernel,
        out_shape=[jax.ShapeDtypeStruct((SHARD, HEADS * DH), bf16)] * (rows.shape[1] // SHARD),
        in_specs=[VMEM],
        out_specs=[VMEM] * (rows.shape[1] // SHARD),
        compiler_params=params(),
    )(rows)


def fold(op, x):
    return op(x.reshape(-1, 8, x.shape[-1]), axis=0)


def online_step(scores, values_t, cols, max_ref, sum_ref, out_ref):
    before = max_ref[0:1, cols]
    highest = jnp.max(fold(jnp.max, scores), axis=0, keepdims=True) * scale_log2
    now = jnp.maximum(before, highest)
    shrink = jnp.exp2(before - now)
    weights = jnp.exp2(scores * scale_log2 - now)
    rounded = weights.astype(bf16)
    block_sum = jnp.sum(fold(jnp.sum, weights), axis=0, keepdims=True)
    sum_ref[0:1, cols] = sum_ref[0:1, cols] * shrink + block_sum
    out_ref[:, cols] = out_ref[:, cols] * shrink + dot(values_t, rounded)
    max_ref[0:1, cols] = now
    return rounded, now


STATE = [(8, ROWS), (8, ROWS), (DH, ROWS)]


def state_shapes():
    return [jax.ShapeDtypeStruct(shape, f32) for shape in STATE]


def open_state(before, after):
    if before:
        for old, new in zip(before, after):
            new[...] = old[...]
    else:
        after[0][...] = jnp.full((8, ROWS), -1e30, f32)
        after[1][...] = jnp.zeros((8, ROWS), f32)
        after[2][...] = jnp.zeros((DH, ROWS), f32)


def await_block(copies, i):
    for k in range(8):

        @pl.when(i == k)
        def _():
            for copy in copies[k:k + 1] if k < 6 else copies[2 * k - 6:2 * k - 4]:
                copy.wait()


def members_of(pieces):
    return sum(piece.shape[0] for piece in pieces)


def load_pieces(pieces, held, sems):
    copies, at = [], 0
    for i, piece in enumerate(pieces):
        members = piece.shape[0]
        copies.append(pltpu.make_async_copy(piece, held.at[pl.ds(at, members)], sems.at[i]))
        at += members
    for copy in copies:
        copy.start()
    return copies


def take(own_ref, other_ref, part, meta_ref):
    rows = slice(part * SHARD, (part + 1) * SHARD)
    own = own_ref[:, rows, :].reshape(HALF, DH)
    other = other_ref[:, rows, :].reshape(HALF, DH)
    own_first = meta_ref[10] > 0
    return jnp.concatenate(
        [jnp.where(own_first, own, other), jnp.where(own_first, other, own)], axis=0
    )


def keys_of(held, i, count=1):
    members = pl.ds(pl.multiple_of(i * MEMBERS, MEMBERS), count * MEMBERS)
    return held[members, :SHARD, :].reshape(count * ROWS, DH)


def values_of(held, i, count=1):
    members = pl.ds(pl.multiple_of(i * MEMBERS, MEMBERS), count * MEMBERS)
    return held[members, SHARD:, :].reshape(count * ROWS, DH)


def keys_of(held, i, count=1):
    members = pl.ds(pl.multiple_of(i * MEMBERS, MEMBERS), count * MEMBERS)
    return held[members, :SHARD, :].reshape(count * ROWS, DH)


def values_of(held, i, count=1):
    members = pl.ds(pl.multiple_of(i * MEMBERS, MEMBERS), count * MEMBERS)
    return held[members, SHARD:, :].reshape(count * ROWS, DH)


def rows_of(i):
    return pl.ds(pl.multiple_of(i * ROWS, ROWS), ROWS)


def teacher_kernel(n_before, n_pieces, last, meta_ref, own_ref, other_ref, *rest):
    before, pieces = rest[:n_before], rest[n_before:n_before + n_pieces]
    rest = rest[n_before + n_pieces:]
    if last:
        target_ref, held, sems = rest[:3]
        state = rest[3:]
    else:
        state, held, sems = rest[:3], rest[3], rest[4]
    copies = load_pieces(pieces, held, sems)
    open_state(before, state)
    queries_t = take(own_ref, other_ref, 0, meta_ref).T

    def step(i, _):
        await_block(copies, 2 * i)
        await_block(copies, 2 * i + 1)
        keys = keys_of(held, 2 * i, 2)
        values_t = values_of(held, 2 * i, 2).T
        for first in (0, HALF):
            cols = slice(first, first + HALF)
            online_step(dot(keys, queries_t[:, cols]), values_t, cols, *state)
        return 0

    lax.fori_loop(0, held.shape[0] // (2 * MEMBERS), step, 0)
    if last:
        target_ref[...] = (state[2][...] / state[1][0:1, :]).astype(bf16)


def teacher(meta, own, other, state, pieces, last=False):
    members = members_of(pieces)
    held = pltpu.VMEM((members, 2 * SHARD, DH), bf16)
    scratch = [held, pltpu.SemaphoreType.DMA((len(pieces),))]
    if last:
        out_shape = [jax.ShapeDtypeStruct((DH, ROWS), bf16)]
        scratch += [pltpu.VMEM(shape, f32) for shape in STATE]
    else:
        out_shape = state_shapes()
    return pl.pallas_call(
        functools.partial(teacher_kernel, len(state), len(pieces), last),
        out_shape=out_shape,
        in_specs=[SMEM, VMEM, VMEM] + [VMEM] * len(state) + [ANY] * len(pieces),
        out_specs=[VMEM] * len(out_shape),
        scratch_shapes=scratch,
        compiler_params=params(),
        cost_estimate=pl.CostEstimate(
            flops=members * 6 * 10**7, bytes_accessed=members * 2**14, transcendentals=0
        ),
    )(meta, own, other, *state, *pieces)


def frames_of(tokens, meta_ref):
    frames = jnp.zeros(tokens.shape, jnp.int32)
    for f in range(6):
        frames = frames + (tokens >= meta_ref[f]).astype(jnp.int32)
    return frames


def groups_seen(meta_ref, last):
    seen = jnp.int32(TOKENS)
    for f in range(6, -1, -1):
        seen = jnp.where(last < meta_ref[f], meta_ref[f], seen)
    return (seen + (ROWS - 1)) // ROWS


def keys_with_frames(keys, group, meta_ref):
    column = lax.broadcasted_iota(jnp.int32, (ROWS, DH), 1)
    tokens = group * ROWS + lax.broadcasted_iota(jnp.int32, (ROWS, DH), 0)
    one_hot = (frames_of(tokens, meta_ref) == column).astype(f32).astype(bf16)
    return jnp.concatenate([keys, one_hot], axis=1)


def by_visibility(meta_ref, group, compute, skip=None):
    seen_early = groups_seen(meta_ref, meta_ref[8] + (HALF - 1))
    seen_late = groups_seen(meta_ref, meta_ref[9] + (HALF - 1))

    @pl.when(group < seen_early)
    def _():
        compute(0)

    @pl.when((group >= seen_early) & (group < seen_late))
    def _():
        compute(HALF)

    if skip is not None:

        @pl.when(group >= seen_late)
        def _():
            skip()


def student_kernel(meta_ref, own_ref, other_ref, target_ref, *rest):
    pieces = rest[:10]
    dq_own_ref, dq_other_ref = rest[10:12]
    outs = rest[12:18]
    held, max_ref, sum_ref, out_ref, weights_ref, max_at, dqt, qt_ref, kv_grad = rest[18:27]
    sems, out_sems = rest[27:]
    copies = load_pieces(pieces, held, sems)
    open_state((), (max_ref, sum_ref, out_ref))
    dqt[...] = jnp.zeros(dqt.shape, f32)
    queries = take(own_ref, other_ref, 1, meta_ref)
    column = lax.broadcasted_iota(jnp.int32, (DH, ROWS), 1)
    row = lax.broadcasted_iota(jnp.int32, (DH, ROWS), 0)
    tokens = jnp.where(column < HALF, meta_ref[8] + column, meta_ref[9] + (column - HALF))
    bias = jnp.where((row > frames_of(tokens, meta_ref)) & (row < 7), hidden_bias, 0.0)
    qt_ref[:DH, :] = queries.T
    qt_ref[DH:, :] = bias.astype(bf16)

    def forward(i, _):
        await_block(copies, i)
        group = meta_ref[16 + i]

        def compute(first):
            rows, cols = rows_of(i), slice(first, ROWS)
            keys = keys_with_frames(keys_of(held, i), group, meta_ref)
            rounded, now = online_step(
                dot(keys, qt_ref[:, cols]), values_of(held, i).T, cols, max_ref, sum_ref, out_ref
            )
            weights_ref[rows, cols] = rounded
            at = pl.ds(pl.multiple_of(i * 8, 8), 8)
            max_at[at, cols] = jnp.broadcast_to(now, (8, ROWS - first))

        by_visibility(meta_ref, group, compute)
        return 0

    lax.fori_loop(0, 8, forward, 0)

    inverse = 1.0 / sum_ref[0:1, :]
    output = out_ref[...] * inverse
    out_grad = (loss_scale * (output - target_ref[...].astype(f32))).astype(bf16).astype(f32)
    delta = jnp.sum(out_grad * output, axis=0, keepdims=True) * inverse
    grad_t = (out_grad * inverse).astype(bf16)
    delta_1 = delta.astype(bf16).astype(f32)
    delta_2 = (delta - delta_1).astype(bf16).astype(f32)
    delta_3 = delta - delta_1 - delta_2
    delta_rows = jnp.where(
        row == 0, -delta_1, jnp.where(row == 1, -delta_2, jnp.where(row == 2, -delta_3, 0.0))
    )
    grad_delta_t = jnp.concatenate([grad_t, delta_rows.astype(bf16)], axis=0)
    grad = grad_t.T
    key_column = lax.broadcasted_iota(jnp.int32, (ROWS, DH), 1)
    ones = jnp.where(key_column < 3, 1.0, 0.0).astype(bf16)

    def backward(i, _):
        group = meta_ref[16 + i]

        def compute(first):
            rows, cols = rows_of(i), slice(first, ROWS)
            values = jnp.concatenate([values_of(held, i), ones], axis=1)
            centred = dot(values, grad_delta_t[:, cols])
            at = pl.ds(pl.multiple_of(i * 8, 8), 8)
            shrink = jnp.exp2(max_at[at, cols][0:1] - max_ref[0:1, cols])
            weights = weights_ref[rows, cols].astype(f32) * shrink
            score_grad = (weights * centred).astype(bf16)
            members = pl.ds(pl.multiple_of(i * MEMBERS, MEMBERS), MEMBERS)
            value_grad = dot(weights.astype(bf16), grad[cols])
            key_grad = dot(score_grad, queries[cols]) * scale
            kv_grad[members, SHARD:, :] = value_grad.astype(bf16).reshape(MEMBERS, SHARD, DH)
            kv_grad[members, :SHARD, :] = key_grad.astype(bf16).reshape(MEMBERS, SHARD, DH)
            dqt[:, cols] += dot(keys_of(held, i).T, score_grad)

        def skip():
            members = pl.ds(pl.multiple_of(i * MEMBERS, MEMBERS), MEMBERS)
            kv_grad[members, :, :] = jnp.zeros((MEMBERS, 2 * SHARD, DH), bf16)

        by_visibility(meta_ref, group, compute, skip)
        return 0

    lax.fori_loop(0, 8, backward, 0)
    out_copies = [
        pltpu.make_async_copy(kv_grad.at[pl.ds(i * MEMBERS, MEMBERS)], out, out_sems.at[k])
        for k, (i, out) in enumerate(
            [(0, outs[0]), (1, outs[1]), (2, outs[2].at[0]), (4, outs[2].at[1])]
            + [(3, outs[3].at[0]), (5, outs[3].at[1]), (6, outs[4]), (7, outs[5])]
        )
    ]
    for copy in out_copies:
        copy.start()
    query_grad = (dqt[...] * scale).T.astype(bf16)
    own_first = meta_ref[10] > 0
    first, second = query_grad[:HALF], query_grad[HALF:]
    shape = (HALF_MEMBERS, SHARD, DH)
    dq_own_ref[...] = jnp.where(own_first, first, second).reshape(shape)
    dq_other_ref[...] = jnp.where(own_first, second, first).reshape(shape)
    for copy in out_copies:
        copy.wait()


def student(meta, own, other, target, pieces):
    half = jax.ShapeDtypeStruct((HALF_MEMBERS, SHARD, DH), bf16)
    one = jax.ShapeDtypeStruct((MEMBERS, 2 * SHARD, DH), bf16)
    two = jax.ShapeDtypeStruct((2, MEMBERS, 2 * SHARD, DH), bf16)
    return pl.pallas_call(
        student_kernel,
        out_shape=[half, half, one, one, two, two, one, one],
        in_specs=[SMEM, VMEM, VMEM, VMEM] + [ANY] * 10,
        out_specs=[VMEM] * 2 + [ANY] * 6,
        scratch_shapes=[
            pltpu.VMEM((8 * MEMBERS, 2 * SHARD, DH), bf16),
            pltpu.VMEM((8, ROWS), f32),
            pltpu.VMEM((8, ROWS), f32),
            pltpu.VMEM((DH, ROWS), f32),
            pltpu.VMEM((TOKENS, ROWS), bf16),
            pltpu.VMEM((64, ROWS), f32),
            pltpu.VMEM((DH, ROWS), f32),
            pltpu.VMEM((2 * DH, ROWS), bf16),
            pltpu.VMEM((8 * MEMBERS, 2 * SHARD, DH), bf16),
            pltpu.SemaphoreType.DMA((10,)),
            pltpu.SemaphoreType.DMA((8,)),
        ],
        compiler_params=params(),
        cost_estimate=pl.CostEstimate(
            flops=26 * 10**9, bytes_accessed=10 * 2**20, transcendentals=ROWS * TOKENS
        ),
    )(meta, own, other, target, *pieces)


def exchange(packed):
    return lax.all_to_all(packed, "seq", split_axis=0, concat_axis=0, tiled=True)


def trade(x):
    return lax.ppermute(x, "blk", [(i, 7 - i) for i in range(8)])


def chip_shift(x, by):
    return lax.ppermute(x, "blk", [(i, ((i // 2 + by) % 4) * 2 + i % 2) for i in range(8)])


def swap_cores(x):
    return lax.ppermute(x, "blk", [(i, i ^ 1) for i in range(8)])


def with_other_core(parts):
    return [x for part in parts for x in (part, swap_cores(part))]


def frame_ends(counted):
    counts = jnp.broadcast_to(jnp.sum(counted.astype(f32), axis=0)[:, None], (8, DH))
    counts = counts + swap_cores(counts)
    counts = counts + chip_shift(counts, 1)
    counts = counts + chip_shift(counts, 2)
    return counts[:, 0].astype(jnp.int32)


def per_device(
    teacher_query,
    teacher_key,
    teacher_value,
    student_query,
    student_key,
    student_value,
    frame_index,
):
    blk = lax.axis_index("blk")
    seq = lax.axis_index("seq")
    tie = lax.optimization_barrier
    arrays = (teacher_key, teacher_value, teacher_query, student_query)
    moved = exchange(pack([x[0] for x in arrays], (frame_index,)))
    student_key, student_value, moved = tie((student_key, student_value, moved))
    student_kv = exchange(pack([student_key[0], student_value[0]]))
    teacher_kv = moved[:, :2 * SHARD]
    early = seq < HALF_MEMBERS
    keep = jnp.where(early, 0, HALF_MEMBERS)

    def half_of(x, at):
        return lax.dynamic_slice_in_dim(x, at, HALF_MEMBERS, axis=0)

    queries = moved[:, 2 * SHARD:4 * SHARD]
    own = half_of(queries, keep)
    other = trade(half_of(queries, HALF_MEMBERS - keep))

    chip, core = blk // 2, blk % 2
    own_start = blk * ROWS + jnp.where(early, 0, HALF)
    other_start = (7 - blk) * ROWS + jnp.where(early, HALF, 0)
    halves = jnp.stack([jnp.minimum(own_start, other_start), jnp.maximum(own_start, other_start)])
    groups = []
    for by in (0, 1, 3, 2):
        groups += [((chip + by) % 4) * 2 + core, ((chip + by) % 4) * 2 + 1 - core]
    own_first = (own_start < other_start).astype(jnp.int32)
    place = [halves, own_first[None], jnp.zeros((5,), jnp.int32), jnp.stack(groups)]
    place = jnp.concatenate([jnp.zeros((8,), jnp.int32)] + place).astype(jnp.int32)

    def near_pieces(after, before):
        return with_other_core([after, before])

    def far_halves(before, after):
        return [chip_shift(before[:HALF_MEMBERS], 1), chip_shift(after[HALF_MEMBERS:], 3)]

    teacher_after, teacher_before = chip_shift(teacher_kv, 3), chip_shift(teacher_kv, 1)
    student_after, student_before = chip_shift(student_kv, 3), chip_shift(student_kv, 1)
    ends = frame_ends(moved[:, 4 * SHARD, :8])
    meta = jnp.concatenate([ends, place[8:]])
    teacher_here = with_other_core([teacher_kv])
    teacher_near = near_pieces(teacher_after, teacher_before)
    teacher_far = far_halves(teacher_before, teacher_after)
    teacher_far += [swap_cores(x) for x in teacher_far]
    student_here = with_other_core([student_kv])
    student_near = near_pieces(student_after, student_before)

    (target,) = teacher(
        place, own, other, [], teacher_here + teacher_near + teacher_far, last=True
    )
    student_before, student_after, target = tie((student_before, student_after, target))
    student_halves = far_halves(student_before, student_after)
    student_far = student_halves + [swap_cores(x) for x in student_halves]
    grads = student(meta, own, other, target, student_here + student_near + student_far)
    query_own, query_other, here_mine, here_other, near_mine, near_other, far_mine, far_other = grads
    far = (far_mine.astype(f32) + swap_cores(far_other).astype(f32)).astype(bf16)
    query_back = trade(query_other)
    by_ahead = chip_shift(far[:HALF_MEMBERS], 1).astype(f32)
    by_behind = chip_shift(far[HALF_MEMBERS:], 3).astype(f32)
    near = near_mine.astype(f32) + swap_cores(near_other).astype(f32)
    ahead = jnp.concatenate([near[0, :HALF_MEMBERS] + by_ahead, near[0, HALF_MEMBERS:]])
    behind = jnp.concatenate([near[1, :HALF_MEMBERS], near[1, HALF_MEMBERS:] + by_behind])
    total = here_mine.astype(f32) + swap_cores(here_other).astype(f32)
    for part in (chip_shift(ahead.astype(bf16), 1), chip_shift(behind.astype(bf16), 3)):
        total = total + part.astype(f32)
    query_grad = jnp.concatenate(
        [jnp.where(early, query_own, query_back), jnp.where(early, query_back, query_own)]
    )
    (query_out,) = unpack(exchange(query_grad))
    key_out, value_out = unpack(exchange(total.astype(bf16)))
    return (query_out[None], key_out[None], value_out[None])


def solution(mesh):
    spec = P("blk", "seq", None)
    return jax.shard_map(
        per_device,
        mesh=mesh,
        in_specs=(spec,) * 6 + (P("blk", "seq"),),
        out_specs=(spec,) * 3,
        check_vma=False,
    )
```

```python
import functools

import jax
import jax.numpy as jnp
from jax import lax
from jax.experimental import pallas as pl
from jax.experimental.pallas import tpu as pltpu
from jax.sharding import PartitionSpec as P

DH = 128
HEADS = 32
SHARD = 32
ROWS = 1024
HALF = 512
TOKENS = 8192
EXTRA = 16
MEMBERS = 32
HALF_MEMBERS = 16
scale = DH ** -0.5
scale_log2 = scale * 1.4426950408889634
loss_scale = 64.0
hidden_bias = -131072.0
f32 = jnp.float32
bf16 = jnp.bfloat16
VMEM = pl.BlockSpec(memory_space=pltpu.VMEM)
SMEM = pl.BlockSpec(memory_space=pltpu.SMEM)
ANY = pl.BlockSpec(memory_space=pl.ANY)


def params():
    return pltpu.CompilerParams(vmem_limit_bytes=60 * 2**20)


def dot(a, b):
    return jnp.dot(a, b, preferred_element_type=f32)


def pack_kernel(count, with_frames, *refs):
    out_ref = refs[-1]
    for h in range(HEADS):
        for n in range(count):
            out_ref[h, n * SHARD:(n + 1) * SHARD, :] = refs[n][:, h * DH:(h + 1) * DH]
    if with_frames:
        column = lax.broadcasted_iota(jnp.int32, (EXTRA, DH), 1)
        counts = jnp.zeros((EXTRA, DH), jnp.int32)
        for k in range(SHARD):
            counts = counts + (refs[count][0, k] <= column).astype(jnp.int32)
        counts = counts.astype(f32).astype(bf16)
        for h in range(HEADS):
            out_ref[h, count * SHARD:, :] = counts


def pack(arrays, frames=()):
    count = len(arrays)
    rows = count * SHARD + EXTRA * len(frames)
    return pl.pallas_call(
        functools.partial(pack_kernel, count, len(frames) > 0),
        out_shape=jax.ShapeDtypeStruct((HEADS, rows, DH), bf16),
        in_specs=[VMEM] * count + [SMEM] * len(frames),
        out_specs=VMEM,
        compiler_params=params(),
    )(*arrays, *frames)


def unpack_kernel(in_ref, *out_refs):
    for h in range(HEADS):
        for n in range(len(out_refs)):
            out_refs[n][:, h * DH:(h + 1) * DH] = in_ref[h, n * SHARD:(n + 1) * SHARD, :]


def unpack(rows):
    return pl.pallas_call(
        unpack_kernel,
        out_shape=[jax.ShapeDtypeStruct((SHARD, HEADS * DH), bf16)] * (rows.shape[1] // SHARD),
        in_specs=[VMEM],
        out_specs=[VMEM] * (rows.shape[1] // SHARD),
        compiler_params=params(),
    )(rows)


def fold(op, x):
    return op(x.reshape(-1, 8, x.shape[-1]), axis=0)


def online_step(scores, values_t, cols, max_ref, sum_ref, out_ref):
    before = max_ref[0:1, cols]
    highest = jnp.max(fold(jnp.max, scores), axis=0, keepdims=True) * scale_log2
    now = jnp.maximum(before, highest)
    shrink = jnp.exp2(before - now)
    weights = jnp.exp2(scores * scale_log2 - now)
    rounded = weights.astype(bf16)
    block_sum = jnp.sum(fold(jnp.sum, weights), axis=0, keepdims=True)
    sum_ref[0:1, cols] = sum_ref[0:1, cols] * shrink + block_sum
    out_ref[:, cols] = out_ref[:, cols] * shrink + dot(values_t, rounded)
    max_ref[0:1, cols] = now
    return rounded, now


STATE = [(8, ROWS), (8, ROWS), (DH, ROWS)]


def state_shapes():
    return [jax.ShapeDtypeStruct(shape, f32) for shape in STATE]


def open_state(before, after):
    if before:
        for old, new in zip(before, after):
            new[...] = old[...]
    else:
        after[0][...] = jnp.full((8, ROWS), -1e30, f32)
        after[1][...] = jnp.zeros((8, ROWS), f32)
        after[2][...] = jnp.zeros((DH, ROWS), f32)


def await_block(copies, i):
    for k in range(8):

        @pl.when(i == k)
        def _():
            for copy in copies[k:k + 1] if k < 6 else copies[2 * k - 6:2 * k - 4]:
                copy.wait()


def members_of(pieces):
    return sum(piece.shape[0] for piece in pieces)


def load_pieces(pieces, held, sems):
    copies, at = [], 0
    for i, piece in enumerate(pieces):
        members = piece.shape[0]
        copies.append(pltpu.make_async_copy(piece, held.at[pl.ds(at, members)], sems.at[i]))
        at += members
    for copy in copies:
        copy.start()
    return copies


def take(own_ref, other_ref, part, meta_ref):
    rows = slice(part * SHARD, (part + 1) * SHARD)
    own = own_ref[:, rows, :].reshape(HALF, DH)
    other = other_ref[:, rows, :].reshape(HALF, DH)
    own_first = meta_ref[10] > 0
    return jnp.concatenate(
        [jnp.where(own_first, own, other), jnp.where(own_first, other, own)], axis=0
    )


def keys_of(held, i, count=1):
    members = pl.ds(pl.multiple_of(i * MEMBERS, MEMBERS), count * MEMBERS)
    return held[members, :SHARD, :].reshape(count * ROWS, DH)


def values_of(held, i, count=1):
    members = pl.ds(pl.multiple_of(i * MEMBERS, MEMBERS), count * MEMBERS)
    return held[members, SHARD:, :].reshape(count * ROWS, DH)


def keys_of(held, i, count=1):
    members = pl.ds(pl.multiple_of(i * MEMBERS, MEMBERS), count * MEMBERS)
    return held[members, :SHARD, :].reshape(count * ROWS, DH)


def values_of(held, i, count=1):
    members = pl.ds(pl.multiple_of(i * MEMBERS, MEMBERS), count * MEMBERS)
    return held[members, SHARD:, :].reshape(count * ROWS, DH)


def rows_of(i):
    return pl.ds(pl.multiple_of(i * ROWS, ROWS), ROWS)


def teacher_kernel(n_before, n_pieces, last, meta_ref, own_ref, other_ref, *rest):
    before, pieces = rest[:n_before], rest[n_before:n_before + n_pieces]
    rest = rest[n_before + n_pieces:]
    if last:
        target_ref, held, sems = rest[:3]
        state = rest[3:]
    else:
        state, held, sems = rest[:3], rest[3], rest[4]
    copies = load_pieces(pieces, held, sems)
    open_state(before, state)
    queries_t = take(own_ref, other_ref, 0, meta_ref).T

    def step(i, _):
        await_block(copies, 2 * i)
        await_block(copies, 2 * i + 1)
        keys = keys_of(held, 2 * i, 2)
        values_t = values_of(held, 2 * i, 2).T
        for first in (0, HALF):
            cols = slice(first, first + HALF)
            online_step(dot(keys, queries_t[:, cols]), values_t, cols, *state)
        return 0

    lax.fori_loop(0, held.shape[0] // (2 * MEMBERS), step, 0)
    if last:
        target_ref[...] = (state[2][...] / state[1][0:1, :]).astype(bf16)


def teacher(meta, own, other, state, pieces, last=False):
    members = members_of(pieces)
    held = pltpu.VMEM((members, 2 * SHARD, DH), bf16)
    scratch = [held, pltpu.SemaphoreType.DMA((len(pieces),))]
    if last:
        out_shape = [jax.ShapeDtypeStruct((DH, ROWS), bf16)]
        scratch += [pltpu.VMEM(shape, f32) for shape in STATE]
    else:
        out_shape = state_shapes()
    return pl.pallas_call(
        functools.partial(teacher_kernel, len(state), len(pieces), last),
        out_shape=out_shape,
        in_specs=[SMEM, VMEM, VMEM] + [VMEM] * len(state) + [ANY] * len(pieces),
        out_specs=[VMEM] * len(out_shape),
        scratch_shapes=scratch,
        compiler_params=params(),
        cost_estimate=pl.CostEstimate(
            flops=members * 6 * 10**7, bytes_accessed=members * 2**14, transcendentals=0
        ),
    )(meta, own, other, *state, *pieces)


def frames_of(tokens, meta_ref):
    frames = jnp.zeros(tokens.shape, jnp.int32)
    for f in range(6):
        frames = frames + (tokens >= meta_ref[f]).astype(jnp.int32)
    return frames


def groups_seen(meta_ref, last):
    seen = jnp.int32(TOKENS)
    for f in range(6, -1, -1):
        seen = jnp.where(last < meta_ref[f], meta_ref[f], seen)
    return (seen + (ROWS - 1)) // ROWS


def keys_with_frames(keys, group, meta_ref):
    column = lax.broadcasted_iota(jnp.int32, (ROWS, DH), 1)
    tokens = group * ROWS + lax.broadcasted_iota(jnp.int32, (ROWS, DH), 0)
    one_hot = (frames_of(tokens, meta_ref) == column).astype(f32).astype(bf16)
    return jnp.concatenate([keys, one_hot], axis=1)


def by_visibility(meta_ref, group, compute, skip=None):
    seen_early = groups_seen(meta_ref, meta_ref[8] + (HALF - 1))
    seen_late = groups_seen(meta_ref, meta_ref[9] + (HALF - 1))

    @pl.when(group < seen_early)
    def _():
        compute(0)

    @pl.when((group >= seen_early) & (group < seen_late))
    def _():
        compute(HALF)

    if skip is not None:

        @pl.when(group >= seen_late)
        def _():
            skip()


def student_kernel(meta_ref, own_ref, other_ref, target_ref, *rest):
    pieces = rest[:10]
    dq_own_ref, dq_other_ref = rest[10:12]
    outs = rest[12:18]
    held, max_ref, sum_ref, out_ref, weights_ref, max_at, dqt, qt_ref, kv_grad = rest[18:27]
    sems, out_sems = rest[27:]
    copies = load_pieces(pieces, held, sems)
    open_state((), (max_ref, sum_ref, out_ref))
    dqt[...] = jnp.zeros(dqt.shape, f32)
    queries = take(own_ref, other_ref, 1, meta_ref)
    column = lax.broadcasted_iota(jnp.int32, (DH, ROWS), 1)
    row = lax.broadcasted_iota(jnp.int32, (DH, ROWS), 0)
    tokens = jnp.where(column < HALF, meta_ref[8] + column, meta_ref[9] + (column - HALF))
    bias = jnp.where((row > frames_of(tokens, meta_ref)) & (row < 7), hidden_bias, 0.0)
    qt_ref[:DH, :] = queries.T
    qt_ref[DH:, :] = bias.astype(bf16)

    def forward(i, _):
        await_block(copies, i)
        group = meta_ref[16 + i]

        def compute(first):
            rows, cols = rows_of(i), slice(first, ROWS)
            keys = keys_with_frames(keys_of(held, i), group, meta_ref)
            rounded, now = online_step(
                dot(keys, qt_ref[:, cols]), values_of(held, i).T, cols, max_ref, sum_ref, out_ref
            )
            weights_ref[rows, cols] = rounded
            at = pl.ds(pl.multiple_of(i * 8, 8), 8)
            max_at[at, cols] = jnp.broadcast_to(now, (8, ROWS - first))

        by_visibility(meta_ref, group, compute)
        return 0

    lax.fori_loop(0, 8, forward, 0)

    inverse = 1.0 / sum_ref[0:1, :]
    output = out_ref[...] * inverse
    out_grad = (loss_scale * (output - target_ref[...].astype(f32))).astype(bf16).astype(f32)
    delta = jnp.sum(out_grad * output, axis=0, keepdims=True) * inverse
    grad_t = (out_grad * inverse).astype(bf16)
    delta_1 = delta.astype(bf16).astype(f32)
    delta_2 = (delta - delta_1).astype(bf16).astype(f32)
    delta_3 = delta - delta_1 - delta_2
    delta_rows = jnp.where(
        row == 0, -delta_1, jnp.where(row == 1, -delta_2, jnp.where(row == 2, -delta_3, 0.0))
    )
    grad_delta_t = jnp.concatenate([grad_t, delta_rows.astype(bf16)], axis=0)
    grad = grad_t.T
    key_column = lax.broadcasted_iota(jnp.int32, (ROWS, DH), 1)
    ones = jnp.where(key_column < 3, 1.0, 0.0).astype(bf16)

    def backward(i, _):
        group = meta_ref[16 + i]

        def compute(first):
            rows, cols = rows_of(i), slice(first, ROWS)
            values = jnp.concatenate([values_of(held, i), ones], axis=1)
            centred = dot(values, grad_delta_t[:, cols])
            at = pl.ds(pl.multiple_of(i * 8, 8), 8)
            shrink = jnp.exp2(max_at[at, cols][0:1] - max_ref[0:1, cols])
            weights = weights_ref[rows, cols].astype(f32) * shrink
            score_grad = (weights * centred).astype(bf16)
            members = pl.ds(pl.multiple_of(i * MEMBERS, MEMBERS), MEMBERS)
            value_grad = dot(weights.astype(bf16), grad[cols])
            key_grad = dot(score_grad, queries[cols]) * scale
            kv_grad[members, SHARD:, :] = value_grad.astype(bf16).reshape(MEMBERS, SHARD, DH)
            kv_grad[members, :SHARD, :] = key_grad.astype(bf16).reshape(MEMBERS, SHARD, DH)
            dqt[:, cols] += dot(keys_of(held, i).T, score_grad)

        def skip():
            members = pl.ds(pl.multiple_of(i * MEMBERS, MEMBERS), MEMBERS)
            kv_grad[members, :, :] = jnp.zeros((MEMBERS, 2 * SHARD, DH), bf16)

        by_visibility(meta_ref, group, compute, skip)
        return 0

    lax.fori_loop(0, 8, backward, 0)
    out_copies = [
        pltpu.make_async_copy(kv_grad.at[pl.ds(i * MEMBERS, MEMBERS)], out, out_sems.at[k])
        for k, (i, out) in enumerate(
            [(0, outs[0]), (1, outs[1]), (2, outs[2].at[0]), (4, outs[2].at[1])]
            + [(3, outs[3].at[0]), (5, outs[3].at[1]), (6, outs[4]), (7, outs[5])]
        )
    ]
    for copy in out_copies:
        copy.start()
    query_grad = (dqt[...] * scale).T.astype(bf16)
    own_first = meta_ref[10] > 0
    first, second = query_grad[:HALF], query_grad[HALF:]
    shape = (HALF_MEMBERS, SHARD, DH)
    dq_own_ref[...] = jnp.where(own_first, first, second).reshape(shape)
    dq_other_ref[...] = jnp.where(own_first, second, first).reshape(shape)
    for copy in out_copies:
        copy.wait()


def student(meta, own, other, target, pieces):
    half = jax.ShapeDtypeStruct((HALF_MEMBERS, SHARD, DH), bf16)
    one = jax.ShapeDtypeStruct((MEMBERS, 2 * SHARD, DH), bf16)
    two = jax.ShapeDtypeStruct((2, MEMBERS, 2 * SHARD, DH), bf16)
    return pl.pallas_call(
        student_kernel,
        out_shape=[half, half, one, one, two, two, one, one],
        in_specs=[SMEM, VMEM, VMEM, VMEM] + [ANY] * 10,
        out_specs=[VMEM] * 2 + [ANY] * 6,
        scratch_shapes=[
            pltpu.VMEM((8 * MEMBERS, 2 * SHARD, DH), bf16),
            pltpu.VMEM((8, ROWS), f32),
            pltpu.VMEM((8, ROWS), f32),
            pltpu.VMEM((DH, ROWS), f32),
            pltpu.VMEM((TOKENS, ROWS), bf16),
            pltpu.VMEM((64, ROWS), f32),
            pltpu.VMEM((DH, ROWS), f32),
            pltpu.VMEM((2 * DH, ROWS), bf16),
            pltpu.VMEM((8 * MEMBERS, 2 * SHARD, DH), bf16),
            pltpu.SemaphoreType.DMA((10,)),
            pltpu.SemaphoreType.DMA((8,)),
        ],
        compiler_params=params(),
        cost_estimate=pl.CostEstimate(
            flops=26 * 10**9, bytes_accessed=10 * 2**20, transcendentals=ROWS * TOKENS
        ),
    )(meta, own, other, target, *pieces)


def exchange(packed):
    return lax.all_to_all(packed, "seq", split_axis=0, concat_axis=0, tiled=True)


def trade(x):
    return lax.ppermute(x, "blk", [(i, 7 - i) for i in range(8)])


def chip_shift(x, by):
    return lax.ppermute(x, "blk", [(i, ((i // 2 + by) % 4) * 2 + i % 2) for i in range(8)])


def swap_cores(x):
    return lax.ppermute(x, "blk", [(i, i ^ 1) for i in range(8)])


def with_other_core(parts):
    return [x for part in parts for x in (part, swap_cores(part))]


def frame_ends(counted):
    counts = jnp.broadcast_to(jnp.sum(counted.astype(f32), axis=0)[:, None], (8, DH))
    counts = counts + swap_cores(counts)
    counts = counts + chip_shift(counts, 1)
    counts = counts + chip_shift(counts, 2)
    return counts[:, 0].astype(jnp.int32)


def per_device(
    teacher_query,
    teacher_key,
    teacher_value,
    student_query,
    student_key,
    student_value,
    frame_index,
):
    blk = lax.axis_index("blk")
    seq = lax.axis_index("seq")
    tie = lax.optimization_barrier
    arrays = (teacher_key, teacher_value, teacher_query, student_query)
    moved = exchange(pack([x[0] for x in arrays]))
    student_key, student_value, moved = tie((student_key, student_value, moved))
    student_moved = exchange(pack([student_key[0], student_value[0]], (frame_index,)))
    student_kv = student_moved[:, :2 * SHARD]
    teacher_kv = moved[:, :2 * SHARD]
    early = seq < HALF_MEMBERS
    keep = jnp.where(early, 0, HALF_MEMBERS)

    def half_of(x, at):
        return lax.dynamic_slice_in_dim(x, at, HALF_MEMBERS, axis=0)

    queries = moved[:, 2 * SHARD:4 * SHARD]
    own = half_of(queries, keep)
    other = trade(half_of(queries, HALF_MEMBERS - keep))

    chip, core = blk // 2, blk % 2
    own_start = blk * ROWS + jnp.where(early, 0, HALF)
    other_start = (7 - blk) * ROWS + jnp.where(early, HALF, 0)
    halves = jnp.stack([jnp.minimum(own_start, other_start), jnp.maximum(own_start, other_start)])
    groups = []
    for by in (0, 1, 3, 2):
        groups += [((chip + by) % 4) * 2 + core, ((chip + by) % 4) * 2 + 1 - core]
    own_first = (own_start < other_start).astype(jnp.int32)
    place = [halves, own_first[None], jnp.zeros((5,), jnp.int32), jnp.stack(groups)]
    place = jnp.concatenate([jnp.zeros((8,), jnp.int32)] + place).astype(jnp.int32)

    def near_pieces(after, before):
        return with_other_core([after, before])

    def far_halves(before, after):
        return [chip_shift(before[:HALF_MEMBERS], 1), chip_shift(after[HALF_MEMBERS:], 3)]

    teacher_after, teacher_before = chip_shift(teacher_kv, 3), chip_shift(teacher_kv, 1)
    student_after, student_before = chip_shift(student_kv, 3), chip_shift(student_kv, 1)
    ends = frame_ends(student_moved[:, 2 * SHARD, :8])
    meta = jnp.concatenate([ends, place[8:]])
    teacher_here = with_other_core([teacher_kv])
    teacher_near = near_pieces(teacher_after, teacher_before)
    teacher_far = far_halves(teacher_before, teacher_after)
    teacher_far += [swap_cores(x) for x in teacher_far]
    student_here = with_other_core([student_kv])
    student_near = near_pieces(student_after, student_before)

    (target,) = teacher(
        place, own, other, [], teacher_here + teacher_near + teacher_far, last=True
    )
    student_before, student_after, target = tie((student_before, student_after, target))
    student_halves = far_halves(student_before, student_after)
    student_far = student_halves + [swap_cores(x) for x in student_halves]
    grads = student(meta, own, other, target, student_here + student_near + student_far)
    query_own, query_other, here_mine, here_other, near_mine, near_other, far_mine, far_other = grads
    far = (far_mine.astype(f32) + swap_cores(far_other).astype(f32)).astype(bf16)
    query_back = trade(query_other)
    by_ahead = chip_shift(far[:HALF_MEMBERS], 1).astype(f32)
    by_behind = chip_shift(far[HALF_MEMBERS:], 3).astype(f32)
    near = near_mine.astype(f32) + swap_cores(near_other).astype(f32)
    ahead = jnp.concatenate([near[0, :HALF_MEMBERS] + by_ahead, near[0, HALF_MEMBERS:]])
    behind = jnp.concatenate([near[1, :HALF_MEMBERS], near[1, HALF_MEMBERS:] + by_behind])
    total = here_mine.astype(f32) + swap_cores(here_other).astype(f32)
    for part in (chip_shift(ahead.astype(bf16), 1), chip_shift(behind.astype(bf16), 3)):
        total = total + part.astype(f32)
    query_grad = jnp.concatenate(
        [jnp.where(early, query_own, query_back), jnp.where(early, query_back, query_own)]
    )
    (query_out,) = unpack(exchange(query_grad))
    key_out, value_out = unpack(exchange(total.astype(bf16)))
    return (query_out[None], key_out[None], value_out[None])


def solution(mesh):
    spec = P("blk", "seq", None)
    return jax.shard_map(
        per_device,
        mesh=mesh,
        in_specs=(spec,) * 6 + (P("blk", "seq"),),
        out_specs=(spec,) * 3,
        check_vma=False,
    )
```

```python
import functools

import jax
import jax.numpy as jnp
from jax import lax
from jax.experimental import pallas as pl
from jax.experimental.pallas import tpu as pltpu
from jax.sharding import PartitionSpec as P

DH = 128
HEADS = 32
SHARD = 32
ROWS = 1024
HALF = 512
TOKENS = 8192
EXTRA = 16
MEMBERS = 32
HALF_MEMBERS = 16
scale = DH ** -0.5
scale_log2 = scale * 1.4426950408889634
loss_scale = 64.0
hidden_bias = -131072.0
f32 = jnp.float32
bf16 = jnp.bfloat16
VMEM = pl.BlockSpec(memory_space=pltpu.VMEM)
SMEM = pl.BlockSpec(memory_space=pltpu.SMEM)
ANY = pl.BlockSpec(memory_space=pl.ANY)


def params():
    return pltpu.CompilerParams(vmem_limit_bytes=60 * 2**20)


def dot(a, b):
    return jnp.dot(a, b, preferred_element_type=f32)


def pack_kernel(count, with_frames, *refs):
    out_ref = refs[-1]
    for h in range(HEADS):
        for n in range(count):
            out_ref[h, n * SHARD:(n + 1) * SHARD, :] = refs[n][:, h * DH:(h + 1) * DH]
    if with_frames:
        column = lax.broadcasted_iota(jnp.int32, (EXTRA, DH), 1)
        counts = jnp.zeros((EXTRA, DH), jnp.int32)
        for k in range(SHARD):
            counts = counts + (refs[count][0, k] <= column).astype(jnp.int32)
        counts = counts.astype(f32).astype(bf16)
        for h in range(HEADS):
            out_ref[h, count * SHARD:, :] = counts


def pack(arrays, frames=()):
    count = len(arrays)
    rows = count * SHARD + EXTRA * len(frames)
    return pl.pallas_call(
        functools.partial(pack_kernel, count, len(frames) > 0),
        out_shape=jax.ShapeDtypeStruct((HEADS, rows, DH), bf16),
        in_specs=[VMEM] * count + [SMEM] * len(frames),
        out_specs=VMEM,
        compiler_params=params(),
    )(*arrays, *frames)


def unpack_kernel(in_ref, *out_refs):
    for h in range(HEADS):
        for n in range(len(out_refs)):
            out_refs[n][:, h * DH:(h + 1) * DH] = in_ref[h, n * SHARD:(n + 1) * SHARD, :]


def unpack(rows):
    return pl.pallas_call(
        unpack_kernel,
        out_shape=[jax.ShapeDtypeStruct((SHARD, HEADS * DH), bf16)] * (rows.shape[1] // SHARD),
        in_specs=[VMEM],
        out_specs=[VMEM] * (rows.shape[1] // SHARD),
        compiler_params=params(),
    )(rows)


def fold(op, x):
    return op(x.reshape(-1, 8, x.shape[-1]), axis=0)


def online_step(scores, values_t, cols, max_ref, sum_ref, out_ref):
    before = max_ref[0:1, cols]
    highest = jnp.max(fold(jnp.max, scores), axis=0, keepdims=True) * scale_log2
    now = jnp.maximum(before, highest)
    shrink = jnp.exp2(before - now)
    weights = jnp.exp2(scores * scale_log2 - now)
    rounded = weights.astype(bf16)
    block_sum = jnp.sum(fold(jnp.sum, weights), axis=0, keepdims=True)
    sum_ref[0:1, cols] = sum_ref[0:1, cols] * shrink + block_sum
    out_ref[:, cols] = out_ref[:, cols] * shrink + dot(values_t, rounded)
    max_ref[0:1, cols] = now
    return rounded, now


STATE = [(8, ROWS), (8, ROWS), (DH, ROWS)]


def state_shapes():
    return [jax.ShapeDtypeStruct(shape, f32) for shape in STATE]


def open_state(before, after):
    if before:
        for old, new in zip(before, after):
            new[...] = old[...]
    else:
        after[0][...] = jnp.full((8, ROWS), -1e30, f32)
        after[1][...] = jnp.zeros((8, ROWS), f32)
        after[2][...] = jnp.zeros((DH, ROWS), f32)


def await_block(copies, i):
    for k in range(8):

        @pl.when(i == k)
        def _():
            for copy in copies[k:k + 1] if k < 6 else copies[2 * k - 6:2 * k - 4]:
                copy.wait()


def members_of(pieces):
    return sum(piece.shape[0] for piece in pieces)


def load_pieces(pieces, held, sems):
    copies, at = [], 0
    for i, piece in enumerate(pieces):
        members = piece.shape[0]
        copies.append(pltpu.make_async_copy(piece, held.at[pl.ds(at, members)], sems.at[i]))
        at += members
    for copy in copies:
        copy.start()
    return copies


def take(own_ref, other_ref, part, meta_ref):
    rows = slice(part * SHARD, (part + 1) * SHARD)
    own = own_ref[:, rows, :].reshape(HALF, DH)
    other = other_ref[:, rows, :].reshape(HALF, DH)
    own_first = meta_ref[10] > 0
    return jnp.concatenate(
        [jnp.where(own_first, own, other), jnp.where(own_first, other, own)], axis=0
    )


def keys_of(held, i, count=1):
    members = pl.ds(pl.multiple_of(i * MEMBERS, MEMBERS), count * MEMBERS)
    return held[members, :SHARD, :].reshape(count * ROWS, DH)


def values_of(held, i, count=1):
    members = pl.ds(pl.multiple_of(i * MEMBERS, MEMBERS), count * MEMBERS)
    return held[members, SHARD:, :].reshape(count * ROWS, DH)


def keys_of(held, i, count=1):
    members = pl.ds(pl.multiple_of(i * MEMBERS, MEMBERS), count * MEMBERS)
    return held[members, :SHARD, :].reshape(count * ROWS, DH)


def values_of(held, i, count=1):
    members = pl.ds(pl.multiple_of(i * MEMBERS, MEMBERS), count * MEMBERS)
    return held[members, SHARD:, :].reshape(count * ROWS, DH)


def rows_of(i):
    return pl.ds(pl.multiple_of(i * ROWS, ROWS), ROWS)


def teacher_kernel(n_before, n_pieces, last, meta_ref, own_ref, other_ref, *rest):
    before, pieces = rest[:n_before], rest[n_before:n_before + n_pieces]
    rest = rest[n_before + n_pieces:]
    if last:
        target_ref, held, sems = rest[:3]
        state = rest[3:]
    else:
        state, held, sems = rest[:3], rest[3], rest[4]
    copies = load_pieces(pieces, held, sems)
    open_state(before, state)
    queries_t = take(own_ref, other_ref, 0, meta_ref).T

    def step(i, _):
        await_block(copies, 2 * i)
        await_block(copies, 2 * i + 1)
        keys = keys_of(held, 2 * i, 2)
        values_t = values_of(held, 2 * i, 2).T
        for first in (0, HALF):
            cols = slice(first, first + HALF)
            online_step(dot(keys, queries_t[:, cols]), values_t, cols, *state)
        return 0

    lax.fori_loop(0, held.shape[0] // (2 * MEMBERS), step, 0)
    if last:
        target_ref[...] = (state[2][...] / state[1][0:1, :]).astype(bf16)


def teacher(meta, own, other, state, pieces, last=False):
    members = members_of(pieces)
    held = pltpu.VMEM((members, 2 * SHARD, DH), bf16)
    scratch = [held, pltpu.SemaphoreType.DMA((len(pieces),))]
    if last:
        out_shape = [jax.ShapeDtypeStruct((DH, ROWS), bf16)]
        scratch += [pltpu.VMEM(shape, f32) for shape in STATE]
    else:
        out_shape = state_shapes()
    return pl.pallas_call(
        functools.partial(teacher_kernel, len(state), len(pieces), last),
        out_shape=out_shape,
        in_specs=[SMEM, VMEM, VMEM] + [VMEM] * len(state) + [ANY] * len(pieces),
        out_specs=[VMEM] * len(out_shape),
        scratch_shapes=scratch,
        compiler_params=params(),
        cost_estimate=pl.CostEstimate(
            flops=members * 6 * 10**7, bytes_accessed=members * 2**14, transcendentals=0
        ),
    )(meta, own, other, *state, *pieces)


def frames_of(tokens, meta_ref):
    frames = jnp.zeros(tokens.shape, jnp.int32)
    for f in range(6):
        frames = frames + (tokens >= meta_ref[f]).astype(jnp.int32)
    return frames


def groups_seen(meta_ref, last):
    seen = jnp.int32(TOKENS)
    for f in range(6, -1, -1):
        seen = jnp.where(last < meta_ref[f], meta_ref[f], seen)
    return (seen + (ROWS - 1)) // ROWS


def keys_with_frames(keys, group, meta_ref):
    column = lax.broadcasted_iota(jnp.int32, (ROWS, DH), 1)
    tokens = group * ROWS + lax.broadcasted_iota(jnp.int32, (ROWS, DH), 0)
    one_hot = (frames_of(tokens, meta_ref) == column).astype(f32).astype(bf16)
    return jnp.concatenate([keys, one_hot], axis=1)


def by_visibility(meta_ref, group, compute, skip=None):
    seen_early = groups_seen(meta_ref, meta_ref[8] + (HALF - 1))
    seen_late = groups_seen(meta_ref, meta_ref[9] + (HALF - 1))

    @pl.when(group < seen_early)
    def _():
        compute(0)

    @pl.when((group >= seen_early) & (group < seen_late))
    def _():
        compute(HALF)

    if skip is not None:

        @pl.when(group >= seen_late)
        def _():
            skip()


def student_kernel(meta_ref, own_ref, other_ref, target_ref, *rest):
    pieces = rest[:10]
    dq_own_ref, dq_other_ref = rest[10:12]
    outs = rest[12:18]
    held, max_ref, sum_ref, out_ref, weights_ref, max_at, dqt, qt_ref, kv_grad = rest[18:27]
    sems, out_sems = rest[27:]
    copies = load_pieces(pieces, held, sems)
    open_state((), (max_ref, sum_ref, out_ref))
    dqt[...] = jnp.zeros(dqt.shape, f32)
    queries = take(own_ref, other_ref, 1, meta_ref)
    column = lax.broadcasted_iota(jnp.int32, (DH, ROWS), 1)
    row = lax.broadcasted_iota(jnp.int32, (DH, ROWS), 0)
    tokens = jnp.where(column < HALF, meta_ref[8] + column, meta_ref[9] + (column - HALF))
    bias = jnp.where((row > frames_of(tokens, meta_ref)) & (row < 7), hidden_bias, 0.0)
    qt_ref[:DH, :] = queries.T
    qt_ref[DH:, :] = bias.astype(bf16)

    def forward(i, _):
        await_block(copies, i)
        group = meta_ref[16 + i]

        def compute(first):
            rows, cols = rows_of(i), slice(first, ROWS)
            keys = keys_with_frames(keys_of(held, i), group, meta_ref)
            rounded, now = online_step(
                dot(keys, qt_ref[:, cols]), values_of(held, i).T, cols, max_ref, sum_ref, out_ref
            )
            weights_ref[rows, cols] = rounded
            at = pl.ds(pl.multiple_of(i * 8, 8), 8)
            max_at[at, cols] = jnp.broadcast_to(now, (8, ROWS - first))

        by_visibility(meta_ref, group, compute)
        return 0

    lax.fori_loop(0, 8, forward, 0)

    inverse = 1.0 / sum_ref[0:1, :]
    output = out_ref[...] * inverse
    out_grad = (loss_scale * (output - target_ref[...].astype(f32))).astype(bf16).astype(f32)
    delta = jnp.sum(out_grad * output, axis=0, keepdims=True) * inverse
    grad_t = (out_grad * inverse).astype(bf16)
    delta_1 = delta.astype(bf16).astype(f32)
    delta_2 = (delta - delta_1).astype(bf16).astype(f32)
    delta_3 = delta - delta_1 - delta_2
    delta_rows = jnp.where(
        row == 0, -delta_1, jnp.where(row == 1, -delta_2, jnp.where(row == 2, -delta_3, 0.0))
    )
    grad_delta_t = jnp.concatenate([grad_t, delta_rows.astype(bf16)], axis=0)
    grad = grad_t.T
    key_column = lax.broadcasted_iota(jnp.int32, (ROWS, DH), 1)
    ones = jnp.where(key_column < 3, 1.0, 0.0).astype(bf16)

    out_copies = [
        pltpu.make_async_copy(kv_grad.at[pl.ds(i * MEMBERS, MEMBERS)], out, out_sems.at[k])
        for k, (i, out) in enumerate(
            [(0, outs[0]), (1, outs[1]), (2, outs[2].at[0]), (4, outs[2].at[1])]
            + [(3, outs[3].at[0]), (5, outs[3].at[1]), (6, outs[4]), (7, outs[5])]
        )
    ]

    def backward(i, _):
        group = meta_ref[16 + i]

        def compute(first):
            rows, cols = rows_of(i), slice(first, ROWS)
            values = jnp.concatenate([values_of(held, i), ones], axis=1)
            centred = dot(values, grad_delta_t[:, cols])
            at = pl.ds(pl.multiple_of(i * 8, 8), 8)
            shrink = jnp.exp2(max_at[at, cols][0:1] - max_ref[0:1, cols])
            weights = weights_ref[rows, cols].astype(f32) * shrink
            score_grad = (weights * centred).astype(bf16)
            members = pl.ds(pl.multiple_of(i * MEMBERS, MEMBERS), MEMBERS)
            value_grad = dot(weights.astype(bf16), grad[cols])
            key_grad = dot(score_grad, queries[cols]) * scale
            kv_grad[members, SHARD:, :] = value_grad.astype(bf16).reshape(MEMBERS, SHARD, DH)
            kv_grad[members, :SHARD, :] = key_grad.astype(bf16).reshape(MEMBERS, SHARD, DH)
            dqt[:, cols] += dot(keys_of(held, i).T, score_grad)

        def skip():
            members = pl.ds(pl.multiple_of(i * MEMBERS, MEMBERS), MEMBERS)
            kv_grad[members, :, :] = jnp.zeros((MEMBERS, 2 * SHARD, DH), bf16)

        by_visibility(meta_ref, group, compute, skip)
        for k, block in enumerate((0, 1, 2, 4, 3, 5, 6, 7)):
            pl.when(i == block)(out_copies[k].start)
        return 0

    lax.fori_loop(0, 8, backward, 0)
    query_grad = (dqt[...] * scale).T.astype(bf16)
    own_first = meta_ref[10] > 0
    first, second = query_grad[:HALF], query_grad[HALF:]
    shape = (HALF_MEMBERS, SHARD, DH)
    dq_own_ref[...] = jnp.where(own_first, first, second).reshape(shape)
    dq_other_ref[...] = jnp.where(own_first, second, first).reshape(shape)
    for copy in out_copies:
        copy.wait()


def student(meta, own, other, target, pieces):
    half = jax.ShapeDtypeStruct((HALF_MEMBERS, SHARD, DH), bf16)
    one = jax.ShapeDtypeStruct((MEMBERS, 2 * SHARD, DH), bf16)
    two = jax.ShapeDtypeStruct((2, MEMBERS, 2 * SHARD, DH), bf16)
    return pl.pallas_call(
        student_kernel,
        out_shape=[half, half, one, one, two, two, one, one],
        in_specs=[SMEM, VMEM, VMEM, VMEM] + [ANY] * 10,
        out_specs=[VMEM] * 2 + [ANY] * 6,
        scratch_shapes=[
            pltpu.VMEM((8 * MEMBERS, 2 * SHARD, DH), bf16),
            pltpu.VMEM((8, ROWS), f32),
            pltpu.VMEM((8, ROWS), f32),
            pltpu.VMEM((DH, ROWS), f32),
            pltpu.VMEM((TOKENS, ROWS), bf16),
            pltpu.VMEM((64, ROWS), f32),
            pltpu.VMEM((DH, ROWS), f32),
            pltpu.VMEM((2 * DH, ROWS), bf16),
            pltpu.VMEM((8 * MEMBERS, 2 * SHARD, DH), bf16),
            pltpu.SemaphoreType.DMA((10,)),
            pltpu.SemaphoreType.DMA((8,)),
        ],
        compiler_params=params(),
        cost_estimate=pl.CostEstimate(
            flops=26 * 10**9, bytes_accessed=10 * 2**20, transcendentals=ROWS * TOKENS
        ),
    )(meta, own, other, target, *pieces)


def exchange(packed):
    return lax.all_to_all(packed, "seq", split_axis=0, concat_axis=0, tiled=True)


def trade(x):
    return lax.ppermute(x, "blk", [(i, 7 - i) for i in range(8)])


def chip_shift(x, by):
    return lax.ppermute(x, "blk", [(i, ((i // 2 + by) % 4) * 2 + i % 2) for i in range(8)])


def swap_cores(x):
    return lax.ppermute(x, "blk", [(i, i ^ 1) for i in range(8)])


def with_other_core(parts):
    return [x for part in parts for x in (part, swap_cores(part))]


def frame_ends(counted):
    counts = jnp.broadcast_to(jnp.sum(counted.astype(f32), axis=0)[:, None], (8, DH))
    counts = counts + swap_cores(counts)
    counts = counts + chip_shift(counts, 1)
    counts = counts + chip_shift(counts, 2)
    return counts[:, 0].astype(jnp.int32)


def per_device(
    teacher_query,
    teacher_key,
    teacher_value,
    student_query,
    student_key,
    student_value,
    frame_index,
):
    blk = lax.axis_index("blk")
    seq = lax.axis_index("seq")
    tie = lax.optimization_barrier
    arrays = (teacher_key, teacher_value, teacher_query, student_query)
    moved = exchange(pack([x[0] for x in arrays], (frame_index,)))
    student_key, student_value, moved = tie((student_key, student_value, moved))
    student_kv = exchange(pack([student_key[0], student_value[0]]))
    teacher_kv = moved[:, :2 * SHARD]
    early = seq < HALF_MEMBERS
    keep = jnp.where(early, 0, HALF_MEMBERS)

    def half_of(x, at):
        return lax.dynamic_slice_in_dim(x, at, HALF_MEMBERS, axis=0)

    queries = moved[:, 2 * SHARD:4 * SHARD]
    own = half_of(queries, keep)
    other = trade(half_of(queries, HALF_MEMBERS - keep))

    chip, core = blk // 2, blk % 2
    own_start = blk * ROWS + jnp.where(early, 0, HALF)
    other_start = (7 - blk) * ROWS + jnp.where(early, HALF, 0)
    halves = jnp.stack([jnp.minimum(own_start, other_start), jnp.maximum(own_start, other_start)])
    groups = []
    for by in (0, 1, 3, 2):
        groups += [((chip + by) % 4) * 2 + core, ((chip + by) % 4) * 2 + 1 - core]
    own_first = (own_start < other_start).astype(jnp.int32)
    place = [halves, own_first[None], jnp.zeros((5,), jnp.int32), jnp.stack(groups)]
    place = jnp.concatenate([jnp.zeros((8,), jnp.int32)] + place).astype(jnp.int32)

    def near_pieces(after, before):
        return with_other_core([after, before])

    def far_halves(before, after):
        return [chip_shift(before[:HALF_MEMBERS], 1), chip_shift(after[HALF_MEMBERS:], 3)]

    teacher_after, teacher_before = chip_shift(teacher_kv, 3), chip_shift(teacher_kv, 1)
    student_after, student_before = chip_shift(student_kv, 3), chip_shift(student_kv, 1)
    ends = frame_ends(moved[:, 4 * SHARD, :8])
    meta = jnp.concatenate([ends, place[8:]])
    teacher_here = with_other_core([teacher_kv])
    teacher_near = near_pieces(teacher_after, teacher_before)
    teacher_far = far_halves(teacher_before, teacher_after)
    teacher_far += [swap_cores(x) for x in teacher_far]
    student_here = with_other_core([student_kv])
    student_near = near_pieces(student_after, student_before)

    (target,) = teacher(
        place, own, other, [], teacher_here + teacher_near + teacher_far, last=True
    )
    student_before, student_after, target = tie((student_before, student_after, target))
    student_halves = far_halves(student_before, student_after)
    student_far = student_halves + [swap_cores(x) for x in student_halves]
    grads = student(meta, own, other, target, student_here + student_near + student_far)
    query_own, query_other, here_mine, here_other, near_mine, near_other, far_mine, far_other = grads
    far = (far_mine.astype(f32) + swap_cores(far_other).astype(f32)).astype(bf16)
    query_back = trade(query_other)
    by_ahead = chip_shift(far[:HALF_MEMBERS], 1).astype(f32)
    by_behind = chip_shift(far[HALF_MEMBERS:], 3).astype(f32)
    near = near_mine.astype(f32) + swap_cores(near_other).astype(f32)
    ahead = jnp.concatenate([near[0, :HALF_MEMBERS] + by_ahead, near[0, HALF_MEMBERS:]])
    behind = jnp.concatenate([near[1, :HALF_MEMBERS], near[1, HALF_MEMBERS:] + by_behind])
    total = here_mine.astype(f32) + swap_cores(here_other).astype(f32)
    for part in (chip_shift(ahead.astype(bf16), 1), chip_shift(behind.astype(bf16), 3)):
        total = total + part.astype(f32)
    query_grad = jnp.concatenate(
        [jnp.where(early, query_own, query_back), jnp.where(early, query_back, query_own)]
    )
    (query_out,) = unpack(exchange(query_grad))
    key_out, value_out = unpack(exchange(total.astype(bf16)))
    return (query_out[None], key_out[None], value_out[None])


def solution(mesh):
    spec = P("blk", "seq", None)
    return jax.shard_map(
        per_device,
        mesh=mesh,
        in_specs=(spec,) * 6 + (P("blk", "seq"),),
        out_specs=(spec,) * 3,
        check_vma=False,
    )
```
